512 devices in a mesh: gx: 4 (over x), gy: 16 (over z_lo, y), gz: 8 (over z_hi, core).
Axes of the slice: x: 4, y: 4, z: 16 (z_hi: 4, z_lo: 4; z = z_hi * 4 + z_lo), core: 2. Of those that a mesh axis runs over, the one named last changes fastest.
Arguments:
- bin_mass: float32 [32, 128, 128, 64], P('gx', 'gy', 'gz'), may hold values from 0.02 to 2
- courant: float32 [3, 32, 128, 128], P(None, 'gx', 'gy', 'gz'), may hold values from 0.05 to 0.3
- sub_courant: float32 [64], replicated, may hold values from 0.3 to 0.9
- fall_steps: int32 [64], replicated, may hold values from 1 to 24, as said below
- frag_gain: bfloat16 [4096, 64], replicated, may hold values from -0.01171875 to 0.01171875
- collide: bfloat16 [64, 64], replicated, may hold values from 0.0019989014 to 0.019897461
Outputs:
- updated_mass: float32 [32, 128, 128, 64], P('gx', 'gy', 'gz')
- rainfall: float32 [32, 128, 64], P('gx', ('gy', 'gz'))
The draws below stay inside these ranges and needn't reach their ends.
Inputs may be any that keep to these rules, and one draw needn't show every extreme that they name: `fall_steps`: some bin takes 24 substeps.
All inputs are finite; a program needn't handle non-finite values.
Results may differ from the reference program's by a relative error of at most 0.003.
Values sent between devices are 32-bit elements; how exact they have to be, the bound alone decides.
A program may use at most 64 MiB of HBM per device.

```python
import math
import jax
import jax.numpy as jnp
from jax import lax

NB = 64
SUBS = 24
NX = 32
NY = 128
NZ = 128


def draw_fall_steps(key, part):
    first_key, second_key = jax.random.split(jax.random.fold_in(key, 17))
    counts = jax.random.randint(first_key, (NB,), 1, SUBS + 1)
    chosen = jax.random.randint(second_key, (), 0, NB)
    return jnp.where(jnp.arange(NB) == chosen, SUBS, counts).astype(jnp.int32)


def block_levels(own_key, shape, cuts, least, high):
    def one(axis_at, blocks):
        draws = jax.random.uniform(jax.random.fold_in(jax.random.fold_in(own_key, 6), axis_at), (blocks,), jnp.float32, least / len(cuts), high / len(cuts))
        return jnp.repeat(jnp.exp(draws), shape[axis_at] // blocks).reshape((-1,) + (1,) * (len(shape) - axis_at - 1))

    gain = one(*cuts[0])
    for cut in cuts[1:]:
        gain = gain * one(*cut)
    return gain


def noise(own_key, shape, width, most, kind=jnp.bfloat16):
    values = width * jax.random.normal(own_key, shape, jnp.float32)
    return jnp.clip(values, min=-most, max=most).astype(kind)


def setup_inputs(seed: int = 0) -> dict:
    splits = jax.random.split(jax.random.key(seed), 7)
    return {
        "bin_mass": jnp.clip(jnp.exp(math.log(2.0) - 4.6051702 * jax.random.uniform(splits[0], (NX, NY, NZ, NB), jnp.float32) ** block_levels(splits[0], (NX, NY, NZ, NB), ((0, 4), (1, 16), (2, 8)), -0.2, 0.2)), 0.02, 2.0),
        "courant": jnp.clip(0.05 + 0.25 * jax.random.uniform(splits[1], (3, NX, NY, NZ), jnp.float32) ** block_levels(splits[1], (3, NX, NY, NZ), ((1, 4), (2, 16), (3, 8)), -0.2, 0.2), 0.05, 0.3),
        "sub_courant": jnp.clip(jax.random.uniform(splits[2], (NB,), jnp.float32, 0.3, 0.9), 0.3, 0.9),
        "fall_steps": draw_fall_steps(jax.random.fold_in(splits[6], 71), 0),
        "frag_gain": noise(splits[4], (NB * NB, NB), (64 * NB * NB) ** -0.5, 0.01171875),
        "collide": jnp.clip(jnp.exp(jax.random.uniform(splits[5], (NB, NB), jnp.float32, math.log(0.0019989014), math.log(0.019897461))), 0.0019989014, 0.019897461).astype(jnp.bfloat16),
    }


EPS = 1e-6


def face_estimate(far_left, near_left, centre, near_right, far_right):
    left_poly = (2.0 * far_left - 7.0 * near_left + 11.0 * centre) / 6.0
    mid_poly = (-near_left + 5.0 * centre + 2.0 * near_right) / 6.0
    right_poly = (2.0 * centre + 5.0 * near_right - far_right) / 6.0
    left_smooth = 13.0 / 12.0 * jnp.square(far_left - 2.0 * near_left + centre) + 0.25 * jnp.square(far_left - 4.0 * near_left + 3.0 * centre)
    mid_smooth = 13.0 / 12.0 * jnp.square(near_left - 2.0 * centre + near_right) + 0.25 * jnp.square(near_left - near_right)
    right_smooth = 13.0 / 12.0 * jnp.square(centre - 2.0 * near_right + far_right) + 0.25 * jnp.square(3.0 * centre - 4.0 * near_right + far_right)
    left_weight = 0.1 / jnp.square(EPS + left_smooth)
    mid_weight = 0.6 / jnp.square(EPS + mid_smooth)
    right_weight = 0.3 / jnp.square(EPS + right_smooth)
    return (left_weight * left_poly + mid_weight * mid_poly + right_weight * right_poly) / (left_weight + mid_weight + right_weight)


def advect(padded, wind_pad):
    change_sum = None
    for axis_d in range(3):
        values_d = padded
        speed_d = wind_pad[axis_d]
        for other in range(3):
            if other != axis_d:
                values_d = lax.slice_in_dim(values_d, 3, values_d.shape[other] - 3, axis=other)
                speed_d = lax.slice_in_dim(speed_d, 1, speed_d.shape[other] - 1, axis=other)
        length = padded.shape[axis_d] - 6
        stencil = [lax.slice_in_dim(values_d, k, k + length + 1, axis=axis_d) for k in range(5)]
        estimate = face_estimate(stencil[0], stencil[1], stencil[2], stencil[3], stencil[4])
        face_speed = 0.5 * (lax.slice_in_dim(speed_d, 0, length + 1, axis=axis_d) + lax.slice_in_dim(speed_d, 1, length + 2, axis=axis_d))
        face_flux = face_speed[..., None] * estimate
        difference = lax.slice_in_dim(face_flux, 1, length + 1, axis=axis_d) - lax.slice_in_dim(face_flux, 0, length, axis=axis_d)
        change_sum = -difference if change_sum is None else change_sum - difference
    return change_sum


def zero_layer(current):
    return jnp.zeros_like(current[:, :, :1])


def settle(mass, sub_courant, fall_steps, top_layer):
    def substep(step, carry):
        current, rainfall = carry
        fall_rate = jnp.where(step < fall_steps, sub_courant, jnp.float32(0.0))
        upper_cell = jnp.concatenate([current[:, :, 1:], top_layer(current)], axis=2)
        rainfall = rainfall + fall_rate * current[:, :, 0]
        current = current + fall_rate * (upper_cell - current)
        return (current, rainfall)

    empty = jnp.zeros((mass.shape[0], mass.shape[1], mass.shape[3]), jnp.float32)
    return lax.fori_loop(0, SUBS, substep, (mass, empty))


def breakup(settled, frag_gain, collide):
    bins = settled.shape[-1]
    flat = settled.reshape(-1, bins)
    count = flat.shape[0]
    block = 512 if count % 512 == 0 else count

    def block_rows(rows_in):
        rounded = rows_in.astype(jnp.bfloat16)
        widened = rounded.astype(jnp.float32)
        pair_terms = (widened[:, :, None] * widened[:, None, :]).reshape(rows_in.shape[0], bins * bins).astype(jnp.bfloat16)
        gained = jnp.dot(pair_terms, frag_gain, preferred_element_type=jnp.float32)
        breakup_loss = jnp.dot(rounded, collide, preferred_element_type=jnp.float32)
        return rows_in + gained - rows_in * breakup_loss

    blocks = flat.reshape(count // block, block, bins)
    return lax.map(block_rows, blocks).reshape(settled.shape)


def reference(bin_mass, courant, sub_courant, fall_steps, frag_gain, collide):
    wind_pad = jnp.pad(courant, ((0, 0), (1, 1), (1, 1), (1, 1)))

    def tendency(values):
        return advect(jnp.pad(values, ((3, 3), (3, 3), (3, 3), (0, 0))), wind_pad)

    section_one = bin_mass + tendency(bin_mass)
    advected = 0.5 * bin_mass + 0.5 * (section_one + tendency(section_one))
    settled, rainfall = settle(advected, sub_courant, fall_steps, zero_layer)
    updated_mass = breakup(settled, frag_gain, collide)
    return updated_mass, rainfall
```

```python
import functools

import jax
import jax.numpy as jnp
from jax import lax
from jax.experimental import pallas as pl
from jax.experimental.pallas import tpu as pltpu
from jax.sharding import PartitionSpec as P

MESH = pl.DeviceIdType.MESH
SUBS = 24
EPS4 = 4e-6
F32 = jnp.float32
BF16 = jnp.bfloat16

OWN = 3 * 32
TOP = 19 * 32
FIELD = 21 * 32
COLUMN = 40 * 8


def weno_line(count, value, speed, emit):
    f_a, f_b, f_c, f_d = value(-3), value(-2), value(-1), value(0)
    d_prev, d_here, d_next = f_b - f_a, f_c - f_b, f_d - f_c
    half_here, half_next = 0.5 * f_c, 0.5 * f_d

    def smooth(e):
        return (13.0 / 3.0) * (e * e) + EPS4

    e_low, e_mid = d_here - d_prev, d_next - d_here
    q_low, q_mid = smooth(e_low), smooth(e_mid)
    t_low = e_mid - e_low
    f_last = f_d
    flux_prev = None
    for face in range(count + 1):
        f_new = value(face + 1)
        d_new = f_new - f_last
        e_high = d_new - d_next
        q_high = smooth(e_high)
        t_high = e_high - e_mid
        g_low = e_low + 2.0 * d_here
        g_mid = d_here + d_next
        g_high = e_high - 2.0 * d_next
        b_low = q_low + g_low * g_low
        b_mid = q_mid + g_mid * g_mid
        b_high = q_high + g_high * g_high
        w_low = b_mid * b_high
        w_mid = b_low * b_high
        w_high = b_low * b_mid
        w_low = w_low * w_low
        w_mid = w_mid * w_mid
        w_high = 0.5 * (w_high * w_high)
        num = w_low * ((1.0 / 3.0) * t_low) + w_high * t_high
        den = w_low + 6.0 * (w_mid + w_high)
        central = (half_here + half_next) - (1.0 / 6.0) * e_mid
        flux = speed(face) * (central - num * pl.reciprocal(den, approx=True))
        if face:
            emit(face - 1, flux - flux_prev)
        flux_prev = flux
        f_last = f_new
        half_here, half_next = half_next, 0.5 * f_new
        d_here, d_next = d_next, d_new
        e_low, e_mid = e_mid, e_high
        q_low, q_mid = q_mid, q_high
        t_low = t_high


def kernel(
    nx, ny, nz,
    mass_ref, courant_ref, rate_ref, steps_ref, gain_ref, collide_ref,
    out_ref, rain_ref,
    raw, gains, field, tend, x_low, x_high, x_out, y_low, y_high, y_out, y_in, winds,
    speed_x, speed_y, speed_z, taps, rain_taps, levels, stage, cells, rounded, pairs, rain,
    load_sem, halo_send, halo_recv, wind_send, wind_recv, sed_send, sed_recv, rain_send, rain_recv,
):
    gx, gy, gz = lax.axis_index("gx"), lax.axis_index("gy"), lax.axis_index("gz")
    odd = lax.rem(gz, 2) == 1

    def when(cond, fn):
        pl.when(cond)(fn)

    sides = [
        (gx > 0, {"gx": lax.rem(gx + nx - 1, nx)}),
        (gx < nx - 1, {"gx": lax.rem(gx + 1, nx)}),
        (gy > 0, {"gy": lax.rem(gy + ny - 1, ny)}),
        (gy < ny - 1, {"gy": lax.rem(gy + 1, ny)}),
        (gz > 0, {"gz": lax.rem(gz + nz - 1, nz)}),
        (gz < nz - 1, {"gz": lax.rem(gz + 1, nz)}),
        (gz > 1, {"gz": lax.rem(gz + nz - 2, nz)}),
        (gz < nz - 2, {"gz": lax.rem(gz + 2, nz)}),
    ]

    barrier = pltpu.get_barrier_semaphore()
    for there, where in sides:
        when(
            there,
            lambda where=where: pl.semaphore_signal(
                barrier, inc=1, device_id=where, device_id_type=MESH
            ),
        )
    mass_load = pltpu.make_async_copy(mass_ref, raw, load_sem.at[0])
    gain_load = pltpu.make_async_copy(gain_ref, gains, load_sem.at[1])
    mass_load.start()
    gain_load.start()

    lane = lax.broadcasted_iota(jnp.int32, (8, 128), 1)
    low = lane < 64

    def turn(v):
        return pltpu.roll(v, 64, 1)

    for d in range(3):
        for y in range(8):
            winds[pl.ds(d * 24 + 8, 8), pl.ds(16 * y, 16)] = courant_ref[d, :, y, :]

    def fill(ref, start, rows):
        ref[pl.ds(start, rows), :] = jnp.zeros((rows, 128), F32)

    def no_x_low():
        fill(x_low, 0, 384)
        fill(winds, 0, 8)

    def no_x_high():
        fill(x_high, 0, 256)
        fill(winds, 16, 8)

    def no_y_low():
        fill(y_in, 0, 384)
        fill(winds, 24, 8)

    def no_y_high():
        fill(y_in, 384, 256)
        fill(winds, 40, 8)

    def no_z_low():
        fill(field, 0, OWN)
        fill(field, FIELD, OWN)
        fill(winds, 48, 8)

    def no_z_high():
        fill(field, TOP, 64)
        fill(field, FIELD + TOP, 64)
        fill(winds, 64, 8)
        for yi in range(4):
            fill(levels, yi * COLUMN + 128, 128)

    for (there, _), fn in zip(
        sides, (no_x_low, no_x_high, no_y_low, no_y_high, no_z_low, no_z_high)
    ):
        when(jnp.logical_not(there), fn)
    def none_above():
        for yi in range(4):
            fill(levels, yi * COLUMN + 256, 64)

    when(gz >= nz - 2, none_above)

    mass_load.wait()

    def pack(z, carry):
        for yi in range(4):
            lo = raw[pl.ds(16 * yi + z, 8, stride=128), :]
            hi = raw[pl.ds(16 * (yi + 4) + z, 8, stride=128), :]
            field[pl.ds(pl.multiple_of(OWN + z * 32 + yi * 8, 8), 8), :] = jnp.concatenate(
                [lo, hi], axis=1
            )
        return carry

    lax.fori_loop(0, 16, pack, 0, unroll=2)

    waits = jnp.int32(0)
    for there, _ in sides:
        waits = waits + there.astype(jnp.int32)
    pl.semaphore_wait(barrier, waits)

    def copy_of(src, dst, send, recv, where):
        return pltpu.make_async_remote_copy(
            src_ref=src, dst_ref=dst, send_sem=send, recv_sem=recv,
            device_id=where, device_id_type=MESH,
        )

    def halos(s):
        base = s * FIELD
        out = []
        spans = [
            (x_out.at[pl.ds(s * 320 + 192, 128)], x_high.at[pl.ds(s * 128, 128)], 0),
            (x_out.at[pl.ds(s * 320, 192)], x_low.at[pl.ds(s * 192, 192)], 1),
            (y_out.at[pl.ds(s * 320 + 192, 128)], y_in.at[pl.ds(384 + s * 128, 128)], 2),
            (y_out.at[pl.ds(s * 320, 192)], y_in.at[pl.ds(s * 192, 192)], 3),
            (field.at[pl.ds(base + OWN, 64)], field.at[pl.ds(base + TOP, 64)], 4),
            (field.at[pl.ds(base + TOP - 96, 96)], field.at[pl.ds(base, 96)], 5),
        ]
        for src, dst, to in spans:
            out.append(
                (to, to ^ 1, copy_of(src, dst, halo_send.at[s, to], halo_recv.at[s, to], sides[to][1]))
            )
        return out

    wind_copies = []
    for d in range(3):
        own = winds.at[pl.ds(d * 24 + 8, 8)]
        for to in (2 * d, 2 * d + 1):
            dst = winds.at[pl.ds(d * 24 + (16 if to == 2 * d else 0), 8)]
            wind_copies.append(
                (to, to ^ 1, copy_of(own, dst, wind_send.at[to], wind_recv.at[to], sides[to][1]))
            )

    def start(copies, only):
        for to, _, copy in copies:
            if to in only:
                when(sides[to][0], copy.start)

    def finish_recv(copies, only):
        for to, source, copy in copies:
            if source in only:
                when(sides[source][0], copy.wait_recv)

    def finish_send(copies):
        for to, _, copy in copies:
            when(sides[to][0], copy.wait_send)

    def pack_x(s):
        base = s * FIELD + OWN
        for k, x in enumerate((5, 6, 7, 0, 1)):
            x_out[pl.ds(s * 320 + k * 64, 64), :] = field[pl.ds(base + x, 64, stride=8), :]

    def pack_y(s):
        base = s * FIELD + OWN

        def body(zi, carry):
            here = base + zi * 32
            for k in range(3):
                lo = field[pl.ds(pl.multiple_of(here + (k + 1) * 8, 8), 8), :]
                hi = field[pl.ds(pl.multiple_of(here + 256 + (k + 1) * 8, 8), 8), :]
                y_out[pl.ds(pl.multiple_of(s * 320 + (zi * 3 + k) * 8, 8), 8), :] = jnp.where(
                    low, turn(lo), hi
                )
            for k in range(2):
                lo = field[pl.ds(pl.multiple_of(here + k * 8, 8), 8), :]
                hi = field[pl.ds(pl.multiple_of(here + 256 + k * 8, 8), 8), :]
                y_out[pl.ds(pl.multiple_of(s * 320 + 192 + (zi * 2 + k) * 8, 8), 8), :] = jnp.where(
                    low, lo, turn(hi)
                )
            return carry

        lax.fori_loop(0, 8, body, 0, unroll=2)

    def send_halos(s):
        copies = halos(s)
        start(copies, (4, 5))
        pack_y(s)
        start(copies, (2, 3))
        pack_x(s)
        start(copies, (0, 1))
        return copies

    def unpack_y(s):
        base = s * FIELD + OWN

        def body(zi, carry):
            here = base + zi * 32
            for k in range(3):
                got = y_in[pl.ds(pl.multiple_of(s * 192 + (zi * 3 + k) * 8, 8), 8), :]
                own_a = turn(field[pl.ds(pl.multiple_of(here + (k + 1) * 8, 8), 8), :])
                own_b = turn(field[pl.ds(pl.multiple_of(here + 256 + (k + 1) * 8, 8), 8), :])
                at = pl.multiple_of((zi * 3 + k) * 8, 8)
                y_low[pl.ds(at, 8), :] = jnp.where(low, got, own_a)
                y_low[pl.ds(at + 192, 8), :] = jnp.where(low, turn(got), own_b)
            for k in range(2):
                got = y_in[pl.ds(pl.multiple_of(384 + s * 128 + (zi * 2 + k) * 8, 8), 8), :]
                own_a = turn(field[pl.ds(pl.multiple_of(here + k * 8, 8), 8), :])
                own_b = turn(field[pl.ds(pl.multiple_of(here + 256 + k * 8, 8), 8), :])
                at = pl.multiple_of((zi * 2 + k) * 8, 8)
                y_high[pl.ds(at, 8), :] = jnp.where(low, own_a, turn(got))
                y_high[pl.ds(at + 128, 8), :] = jnp.where(low, own_b, got)
            return carry

        lax.fori_loop(0, 8, body, 0, unroll=2)

    def pass_x(s):
        base = s * FIELD + OWN

        def body(p, carry):
            at = pl.multiple_of(p * 16, 16)

            def value(i):
                if i < 0:
                    return x_low[pl.ds(s * 192 + (i + 3) * 64 + at, 16), :]
                if i > 7:
                    return x_high[pl.ds(s * 128 + (i - 8) * 64 + at, 16), :]
                return field[pl.ds(base + p * 128 + i, 16, stride=8), :]

            def speed(k):
                return speed_x[pl.ds(k * 64 + at, 16), :]

            def emit(i, change):
                tend[pl.ds(p * 128 + i, 16, stride=8), :] = -change

            weno_line(8, value, speed, emit)
            return carry

        lax.fori_loop(0, 4, body, 0)

    def pass_y(s):
        base = s * FIELD + OWN

        def body(z, carry):
            def value(i):
                if i < 0:
                    return y_low[pl.ds(pl.multiple_of((z * 3 + i + 3) * 8, 8), 8), :]
                if i > 3:
                    return y_high[pl.ds(pl.multiple_of((z * 2 + i - 4) * 8, 8), 8), :]
                return field[pl.ds(pl.multiple_of(base + z * 32 + i * 8, 8), 8), :]

            def speed(k):
                return speed_y[pl.ds(pl.multiple_of((z * 5 + k) * 8, 8), 8), :]

            def emit(i, change):
                at = pl.ds(pl.multiple_of(z * 32 + i * 8, 8), 8)
                tend[at, :] = tend[at, :] - change

            weno_line(4, value, speed, emit)
            return carry

        lax.fori_loop(0, 16, body, 0, unroll=2)

    def pass_z(s, p):
        at = pl.multiple_of(p * 16, 16)

        def value(i):
            return field[pl.ds(s * FIELD + (i + 3) * 32 + at, 16), :]

        def speed(k):
            return speed_z[pl.ds(k * 32 + at, 16), :]

        def emit(i, change):
            stepped = value(i) + (tend[pl.ds(i * 32 + at, 16), :] - change)
            if s == 0:
                field[pl.ds(FIELD + OWN + i * 32 + at, 16), :] = stepped
            else:
                before = field[pl.ds(OWN + i * 32 + at, 16), :]
                settled = 0.5 * before + 0.5 * stepped
                for k in range(2):
                    levels[pl.ds((2 * p + k) * COLUMN + i * 8, 8), :] = settled[8 * k : 8 * k + 8]

        weno_line(16, value, speed, emit)

    start(wind_copies, (4, 5))
    first = send_halos(0)
    start(wind_copies, (0, 1, 2, 3))

    rates = jnp.concatenate([rate_ref[...], rate_ref[...]], axis=1)
    counts = jnp.concatenate([steps_ref[...], steps_ref[...]], axis=1)
    tap = (lax.broadcasted_iota(jnp.int32, (32, 128), 0) == 0).astype(F32)
    fallen = jnp.zeros((32, 128), F32)
    for s in range(SUBS):
        rate = jnp.where(s < counts, rates, 0.0)
        fallen = fallen + rate * tap
        tap = tap + rate * (pltpu.roll(tap, 1, 0) - tap)
    taps[...] = tap
    rain_taps[...] = fallen

    column = jnp.where(low, 0, 64)

    def spread(v, index):
        return jnp.take_along_axis(v, index, axis=1)

    def speeds_x():
        right = 0.5 * (winds[pl.ds(8, 8), :] + winds[pl.ds(9, 8), :])
        left = jnp.broadcast_to(0.5 * (winds[pl.ds(7, 1), :] + winds[pl.ds(8, 1), :]), (8, 128))

        def body(z, carry):
            for yi in range(4):
                index = column + (16 * yi + z)
                row = z * 4 + yi
                speed_x[pl.ds(64 + row, 8, stride=64), :] = spread(right, index)
                speed_x[pl.ds(row, 1), :] = spread(left, index)[0:1, :]
            return carry

        lax.fori_loop(0, 16, body, 0, unroll=2)

    def speeds_y():
        own, before, after = (winds[pl.ds(24 + k, 8), :] for k in (8, 0, 16))
        following = jnp.where(lane < 112, pltpu.roll(own, 112, 1), pltpu.roll(after, 112, 1))
        right = 0.5 * (own + following)
        left = 0.5 * (own + pltpu.roll(before, 16, 1))

        def body(z, carry):
            first_face = jnp.where(
                low,
                spread(left, jnp.zeros_like(lane) + z),
                spread(right, jnp.zeros_like(lane) + (48 + z)),
            )
            speed_y[pl.ds(pl.multiple_of(z * 40, 8), 8), :] = first_face
            for k in range(1, 5):
                speed_y[pl.ds(pl.multiple_of(z * 40 + k * 8, 8), 8), :] = spread(
                    right, column + (16 * (k - 1) + z)
                )
            return carry

        lax.fori_loop(0, 16, body, 0, unroll=2)

    def speeds_z():
        own, before, after = (winds[pl.ds(48 + k, 8), :] for k in (8, 0, 16))
        following = jnp.where(
            lax.rem(lane, 16) == 15, pltpu.roll(after, 15, 1), pltpu.roll(own, 127, 1)
        )
        right = 0.5 * (own + following)
        left = 0.5 * (own + pltpu.roll(before, 113, 1))
        for yi in range(4):
            speed_z[pl.ds(yi * 8, 8), :] = spread(left, column + 16 * yi)

        def body(z, carry):
            for yi in range(4):
                speed_z[pl.ds(pl.multiple_of(32 + z * 32 + yi * 8, 8), 8), :] = spread(
                    right, column + (16 * yi + z)
                )
            return carry

        lax.fori_loop(0, 16, body, 0, unroll=2)

    finish_recv(wind_copies, (0, 1))
    speeds_x()
    finish_recv(first, (0, 1))
    pass_x(0)
    finish_recv(wind_copies, (2, 3))
    speeds_y()
    finish_recv(first, (2, 3))
    unpack_y(0)
    pass_y(0)
    finish_recv(wind_copies, (4, 5))
    speeds_z()
    finish_recv(first, (4, 5))
    for p in range(2):
        pass_z(0, p)

    second = send_halos(1)
    finish_recv(second, (0, 1))
    pass_x(1)
    finish_recv(second, (2, 3))
    unpack_y(1)
    pass_y(1)
    finish_recv(second, (4, 5))

    def sed_copy(kind, yi):
        source, target, side = ((0, 16, 4), (8, 24, 4), (0, 32, 6), (16, 32, 4))[kind]
        return copy_of(
            levels.at[pl.ds(yi * COLUMN + source * 8, 64)],
            levels.at[pl.ds(yi * COLUMN + target * 8, 64)],
            sed_send.at[yi, kind], sed_recv.at[yi, min(kind, 2)], sides[side][1],
        )

    above = gz < nz - 1
    above_two = gz < nz - 2
    sends = (gz > 0, gz > 0, jnp.logical_and(odd, gz > 1), jnp.logical_and(odd, above))

    def sed_start(kind, yi):
        when(sends[kind], sed_copy(kind, yi).start)

    for p in range(2):
        pass_z(1, p)
        for yi in (2 * p, 2 * p + 1):
            sed_start(0, yi)
    for yi in range(4):
        sed_start(1, yi)
        sed_start(2, yi)
    for yi in range(4):
        when(above, sed_copy(0, yi).wait_recv)
        sed_start(3, yi)

    def rain_copy(step):
        side = sides[5] if step == 0 else sides[7]
        return copy_of(rain, rain, rain_send.at[step], rain_recv.at[0], side[1])

    def rain_pass():
        rain_copy(0).start()
        when(above_two, rain_copy(1).start)

    def rain_make():
        def body(yi, carry):
            total = jnp.zeros((8, 128), F32)
            for m in range(SUBS):
                at = pl.ds(pl.multiple_of(yi * COLUMN + m * 8, 8), 8)
                total = total + rain_taps[pl.ds(m, 1), :] * levels[at, :]
            rain[pl.ds(pl.multiple_of(yi * 8, 8), 8), :] = total
            return carry

        lax.fori_loop(0, 4, body, 0)
        rain_pass()

    when(gz == 0, rain_make)

    def rain_forward():
        rain_copy(0).wait_recv()
        rain_pass()

    gain_load.wait()

    def settle(yi, carry):
        def body(group, inner):
            base = yi * COLUMN + group * 64
            sums = [None] * 8
            for j in range(8 + SUBS):
                v = levels[pl.ds(pl.multiple_of(base + j * 8, 8), 8), :]
                for k in range(8):
                    if 0 <= j - k <= SUBS:
                        term = taps[pl.ds(j - k, 1), :] * v
                        sums[k] = term if sums[k] is None else sums[k] + term
            for k in range(8):
                stage[pl.ds(pl.multiple_of(group * 64 + k * 8, 8), 8), :] = sums[k]
            return inner

        lax.fori_loop(0, 2, body, 0)
        return carry

    def breakup(yi):
        block = jnp.concatenate([stage[pl.ds(x, 16, stride=8), :] for x in range(8)], axis=0).T
        for h in range(2):
            cells[:, 128 * h : 128 * h + 128] = block[64 * h : 64 * h + 64]
        small = cells[...].astype(BF16)
        rounded[...] = small.astype(F32)

        def body(i, carry):
            term = rounded[pl.ds(i, 1), :] * rounded[...]
            pairs[pl.ds(pl.multiple_of(i * 64, 64), 64), :] = term.astype(BF16)
            return carry

        lax.fori_loop(0, 64, body, 0, unroll=4)
        gained = jnp.dot(gains[...], pairs[...], preferred_element_type=F32)
        loss = lax.dot_general(
            collide_ref[...], small, (((0,), (0,)), ((), ())), preferred_element_type=F32
        )
        settled = cells[...]
        result = settled + gained - settled * loss
        for h in range(2):
            back = result[:, 128 * h : 128 * h + 128].T
            out_ref[:, 4 * h + yi] = back.reshape(8, 16, 64)

    for yi in range(4):
        when(above, sed_copy(1, yi).wait_recv)
        when(above_two, sed_copy(2, yi).wait_recv)
        settle(yi, 0)
        breakup(yi)
        if yi < 3:
            when(gz == 2 * yi + 2, rain_forward)

    when(odd, rain_copy(0).wait_recv)
    mine = rain[pl.ds(pl.multiple_of(lax.rem(gz, 4) * 8, 8), 8), :]
    upper = (jnp.zeros((8, 128), jnp.int32) + gz) >= 4
    rain_ref[:, 0, :] = jnp.where(upper, turn(mine), mine)[:, :64]

    when(jnp.logical_not(odd), rain_copy(0).wait_send)
    when(jnp.logical_and(jnp.logical_not(odd), above_two), rain_copy(1).wait_send)
    for yi in range(4):
        for kind in range(4):
            when(sends[kind], sed_copy(kind, yi).wait_send)
    finish_send(wind_copies)
    finish_send(first)
    finish_send(second)


def per_device(sizes, bin_mass, courant, sub_courant, fall_steps, frag_gain, collide):
    vmem, dma = pltpu.VMEM, pltpu.SemaphoreType.DMA
    out, rain = pl.pallas_call(
        functools.partial(kernel, *sizes),
        out_shape=(
            jax.ShapeDtypeStruct((8, 8, 16, 64), F32),
            jax.ShapeDtypeStruct((8, 1, 64), F32),
        ),
        in_specs=[
            pl.BlockSpec(memory_space=pl.ANY),
            pl.BlockSpec(memory_space=vmem),
            pl.BlockSpec(memory_space=vmem),
            pl.BlockSpec(memory_space=vmem),
            pl.BlockSpec(memory_space=pl.ANY),
            pl.BlockSpec(memory_space=vmem),
        ],
        out_specs=(pl.BlockSpec(memory_space=vmem), pl.BlockSpec(memory_space=vmem)),
        scratch_shapes=[
            vmem((1024, 64), F32),
            vmem((64, 4096), BF16),
            vmem((2 * FIELD, 128), F32),
            vmem((512, 128), F32),
            vmem((384, 128), F32),
            vmem((256, 128), F32),
            vmem((640, 128), F32),
            vmem((384, 128), F32),
            vmem((256, 128), F32),
            vmem((640, 128), F32),
            vmem((640, 128), F32),
            vmem((72, 128), F32),
            vmem((9 * 64, 128), F32),
            vmem((16 * 40, 128), F32),
            vmem((17 * 32, 128), F32),
            vmem((32, 128), F32),
            vmem((32, 128), F32),
            vmem((4 * COLUMN, 128), F32),
            vmem((128, 128), F32),
            vmem((64, 256), F32),
            vmem((64, 256), F32),
            vmem((4096, 256), BF16),
            vmem((32, 128), F32),
            dma((2,)),
            dma((2, 6)),
            dma((2, 6)),
            dma((6,)),
            dma((6,)),
            dma((4, 4)),
            dma((4, 3)),
            dma((2,)),
            dma((1,)),
        ],
        compiler_params=pltpu.CompilerParams(
            collective_id=0, has_side_effects=True, vmem_limit_bytes=40 << 20
        ),
    )(
        bin_mass.reshape(1024, 64),
        courant,
        sub_courant.reshape(1, 64),
        fall_steps.reshape(1, 64),
        frag_gain.T,
        collide,
    )
    return out, rain


def solution(mesh):
    in_specs = (P("gx", "gy", "gz", None), P(None, "gx", "gy", "gz"), P(), P(), P(), P())
    out_specs = (P("gx", "gy", "gz", None), P("gx", ("gy", "gz"), None))
    sizes = tuple(mesh.shape[a] for a in ("gx", "gy", "gz"))
    return jax.shard_map(
        functools.partial(per_device, sizes),
        mesh=mesh,
        in_specs=in_specs,
        out_specs=out_specs,
        check_vma=False,
    )
```

```python
import functools

import jax
import jax.numpy as jnp
from jax import lax
from jax.experimental import pallas as pl
from jax.experimental.pallas import tpu as pltpu
from jax.sharding import PartitionSpec as P

MESH = pl.DeviceIdType.MESH
SUBS = 24
EPS4 = 4e-6
F32 = jnp.float32
BF16 = jnp.bfloat16

OWN = 3 * 32
TOP = 19 * 32
FIELD = 21 * 32
COLUMN = 40 * 8


def weno_line(count, value, speed, emit):
    f_a, f_b, f_c, f_d = value(-3), value(-2), value(-1), value(0)
    d_prev, d_here, d_next = f_b - f_a, f_c - f_b, f_d - f_c
    half_here, half_next = 0.5 * f_c, 0.5 * f_d

    def smooth(e):
        return (13.0 / 3.0) * (e * e) + EPS4

    e_low, e_mid = d_here - d_prev, d_next - d_here
    q_low, q_mid = smooth(e_low), smooth(e_mid)
    t_low = e_mid - e_low
    f_last = f_d
    flux_prev = None
    for face in range(count + 1):
        f_new = value(face + 1)
        d_new = f_new - f_last
        e_high = d_new - d_next
        q_high = smooth(e_high)
        t_high = e_high - e_mid
        g_low = e_low + 2.0 * d_here
        g_mid = d_here + d_next
        g_high = e_high - 2.0 * d_next
        b_low = q_low + g_low * g_low
        b_mid = q_mid + g_mid * g_mid
        b_high = q_high + g_high * g_high
        w_low = b_mid * b_high
        w_mid = b_low * b_high
        w_high = b_low * b_mid
        w_low = w_low * w_low
        w_mid = w_mid * w_mid
        w_high = 0.5 * (w_high * w_high)
        num = w_low * ((1.0 / 3.0) * t_low) + w_high * t_high
        den = w_low + 6.0 * (w_mid + w_high)
        central = (half_here + half_next) - (1.0 / 6.0) * e_mid
        flux = speed(face) * (central - num * pl.reciprocal(den, approx=True))
        if face:
            emit(face - 1, flux - flux_prev)
        flux_prev = flux
        f_last = f_new
        half_here, half_next = half_next, 0.5 * f_new
        d_here, d_next = d_next, d_new
        e_low, e_mid = e_mid, e_high
        q_low, q_mid = q_mid, q_high
        t_low = t_high


def kernel(
    nx, ny, nz,
    mass_hbm, courant_hbm, rate_hbm, steps_hbm, gain_hbm, collide_hbm,
    out_ref, rain_ref,
    raw, courant_ref, rate_ref, steps_ref, gains, collide_ref, field, tend, x_low, x_high, x_out, y_low, y_high, y_out, y_in, winds,
    speed_x, speed_y, speed_z, taps, rain_taps, levels, stage, cells, rounded, rain,
    load_sem, halo_send, halo_recv, wind_send, wind_recv, sed_send, sed_recv, rain_send, rain_recv,
):
    gx, gy, gz = lax.axis_index("gx"), lax.axis_index("gy"), lax.axis_index("gz")
    parity = lax.rem(gz, 2)
    odd = parity == 1
    even = parity == 0
    near_half, far_half = 1 - parity, parity

    def when(cond, fn):
        pl.when(cond)(fn)

    sides = [
        (gx > 0, {"gx": lax.rem(gx + nx - 1, nx)}),
        (gx < nx - 1, {"gx": lax.rem(gx + 1, nx)}),
        (gy > 0, {"gy": lax.rem(gy + ny - 1, ny)}),
        (gy < ny - 1, {"gy": lax.rem(gy + 1, ny)}),
        (gz > 0, {"gz": lax.rem(gz + nz - 1, nz)}),
        (gz < nz - 1, {"gz": lax.rem(gz + 1, nz)}),
    ]

    barrier = pltpu.get_barrier_semaphore()
    for there, where in sides:
        when(
            there,
            lambda where=where: pl.semaphore_signal(
                barrier, inc=1, device_id=where, device_id_type=MESH
            ),
        )
    loads = [
        pltpu.make_async_copy(source, target, load_sem.at[k])
        for k, (source, target) in enumerate(
            (
                (mass_hbm, raw),
                (courant_hbm, courant_ref),
                (rate_hbm, rate_ref),
                (steps_hbm, steps_ref),
                (gain_hbm, gains),
                (collide_hbm, collide_ref),
            )
        )
    ]
    for load in loads:
        load.start()

    lane = lax.broadcasted_iota(jnp.int32, (8, 128), 1)
    low = lane < 64

    def turn(v):
        return pltpu.roll(v, 64, 1)

    def fill(ref, start, rows):
        ref[pl.ds(start, rows), :] = jnp.zeros((rows, 128), F32)

    def no_x_low():
        fill(x_low, 0, 384)
        fill(winds, 0, 8)

    def no_x_high():
        fill(x_high, 0, 256)
        fill(winds, 16, 8)

    def no_y_low():
        fill(y_in, 0, 384)
        fill(winds, 24, 8)

    def no_y_high():
        fill(y_in, 384, 256)
        fill(winds, 40, 8)

    def no_z_low():
        fill(field, 0, OWN)
        fill(field, FIELD, OWN)
        fill(winds, 48, 8)

    def no_z_high():
        fill(field, TOP, 64)
        fill(field, FIELD + TOP, 64)
        fill(winds, 64, 8)
        for yi in range(4):
            fill(levels, yi * COLUMN + 128, 128)

    for (there, _), fn in zip(
        sides, (no_x_low, no_x_high, no_y_low, no_y_high, no_z_low, no_z_high)
    ):
        when(jnp.logical_not(there), fn)
    def none_above():
        for yi in range(4):
            fill(levels, yi * COLUMN + 256, 64)

    when(gz >= nz - 2, none_above)

    loads[0].wait()

    def pack(z, carry):
        for yi in range(4):
            lo = raw[pl.ds(16 * yi + z, 8, stride=128), :]
            hi = raw[pl.ds(16 * (yi + 4) + z, 8, stride=128), :]
            field[pl.ds(pl.multiple_of(OWN + z * 32 + yi * 8, 8), 8), :] = jnp.concatenate(
                [lo, hi], axis=1
            )
        return carry

    lax.fori_loop(0, 16, pack, 0, unroll=2)

    loads[1].wait()
    for d in range(3):
        for y in range(8):
            winds[pl.ds(d * 24 + 8, 8), pl.ds(16 * y, 16)] = courant_ref[d, :, y, :]

    waits = jnp.int32(0)
    for there, _ in sides:
        waits = waits + there.astype(jnp.int32)
    pl.semaphore_wait(barrier, waits)

    def copy_of(src, dst, send, recv, where):
        return pltpu.make_async_remote_copy(
            src_ref=src, dst_ref=dst, send_sem=send, recv_sem=recv,
            device_id=where, device_id_type=MESH,
        )

    def halo(s, slot, to, src, dst):
        return (
            to,
            to ^ 1,
            copy_of(src, dst, halo_send.at[slot, to], halo_recv.at[slot, to], sides[to][1]),
        )

    def halos_xy(s, slot, half, halves):
        def at(start, rows):
            return pl.ds(pl.multiple_of(start + half * rows, 8), rows * halves)

        return [
            halo(s, slot, 0, x_out.at[at(s * 320 + 192, 64)], x_high.at[at(s * 128, 64)]),
            halo(s, slot, 1, x_out.at[at(s * 320, 96)], x_low.at[at(s * 192, 96)]),
            halo(s, slot, 2, y_out.at[at(s * 320 + 192, 64)], y_in.at[at(384 + s * 128, 64)]),
            halo(s, slot, 3, y_out.at[at(s * 320, 96)], y_in.at[at(s * 192, 96)]),
        ]

    def halos_z(s):
        base = s * FIELD
        return [
            halo(s, s, 4, field.at[pl.ds(base + OWN, 64)], field.at[pl.ds(base + TOP, 64)]),
            halo(s, s, 5, field.at[pl.ds(base + TOP - 96, 96)], field.at[pl.ds(base, 96)]),
        ]

    wind_copies = []
    for d in range(3):
        own = winds.at[pl.ds(d * 24 + 8, 8)]
        for to in (2 * d, 2 * d + 1):
            dst = winds.at[pl.ds(d * 24 + (16 if to == 2 * d else 0), 8)]
            wind_copies.append(
                (to, to ^ 1, copy_of(own, dst, wind_send.at[to], wind_recv.at[to], sides[to][1]))
            )

    def start(copies, only):
        for to, _, copy in copies:
            if to in only:
                when(sides[to][0], copy.start)

    def finish_recv(copies, only):
        for to, source, copy in copies:
            if source in only:
                when(sides[source][0], copy.wait_recv)

    def finish_send(copies):
        for to, _, copy in copies:
            when(sides[to][0], copy.wait_send)

    def by_parity(even_side, fn):
        when(even, lambda: fn((even_side,)))
        when(odd, lambda: fn((9 - even_side,)))

    def start_near(copies):
        by_parity(5, lambda only: start(copies, only))

    def start_far(copies):
        by_parity(4, lambda only: start(copies, only))

    def recv_near(copies):
        by_parity(5, lambda only: finish_recv(copies, only))

    def recv_far(copies):
        by_parity(4, lambda only: finish_recv(copies, only))

    def pack_x(s, half):
        base = s * FIELD + OWN + half * 256
        for k in range(3):
            x_out[pl.ds(pl.multiple_of(s * 320 + half * 96 + k * 32, 8), 32), :] = field[
                pl.ds(base + 5 + k, 32, stride=8), :
            ]
        for k in range(2):
            x_out[pl.ds(pl.multiple_of(s * 320 + 192 + half * 64 + k * 32, 8), 32), :] = field[
                pl.ds(base + k, 32, stride=8), :
            ]

    def pack_y(s, half):
        base = s * FIELD + OWN + half * 256
        for zi in range(4):
            here = base + zi * 32
            for k in range(3):
                lo = field[pl.ds(pl.multiple_of(here + (k + 1) * 8, 8), 8), :]
                hi = field[pl.ds(pl.multiple_of(here + 128 + (k + 1) * 8, 8), 8), :]
                at = s * 320 + half * 96 + (zi * 3 + k) * 8
                y_out[pl.ds(pl.multiple_of(at, 8), 8), :] = jnp.where(low, turn(lo), hi)
            for k in range(2):
                lo = field[pl.ds(pl.multiple_of(here + k * 8, 8), 8), :]
                hi = field[pl.ds(pl.multiple_of(here + 128 + k * 8, 8), 8), :]
                at = s * 320 + 192 + half * 64 + (zi * 2 + k) * 8
                y_out[pl.ds(pl.multiple_of(at, 8), 8), :] = jnp.where(low, lo, turn(hi))

    def unpack_y(s, half):
        base = s * FIELD + OWN + half * 256
        for zi in range(4):
            here = base + zi * 32
            for k in range(3):
                at = half * 96 + (zi * 3 + k) * 8
                got = y_in[pl.ds(pl.multiple_of(s * 192 + at, 8), 8), :]
                own_a = turn(field[pl.ds(pl.multiple_of(here + (k + 1) * 8, 8), 8), :])
                own_b = turn(field[pl.ds(pl.multiple_of(here + 128 + (k + 1) * 8, 8), 8), :])
                at = half * 192 + (zi * 3 + k) * 8
                y_low[pl.ds(pl.multiple_of(at, 8), 8), :] = jnp.where(low, got, own_a)
                y_low[pl.ds(pl.multiple_of(at + 96, 8), 8), :] = jnp.where(low, turn(got), own_b)
            for k in range(2):
                at = 384 + s * 128 + half * 64 + (zi * 2 + k) * 8
                got = y_in[pl.ds(pl.multiple_of(at, 8), 8), :]
                own_a = turn(field[pl.ds(pl.multiple_of(here + k * 8, 8), 8), :])
                own_b = turn(field[pl.ds(pl.multiple_of(here + 128 + k * 8, 8), 8), :])
                at = half * 128 + (zi * 2 + k) * 8
                y_high[pl.ds(pl.multiple_of(at, 8), 8), :] = jnp.where(low, own_a, turn(got))
                y_high[pl.ds(pl.multiple_of(at + 64, 8), 8), :] = jnp.where(low, own_b, got)

    def pass_x(s, half):
        base = s * FIELD + OWN

        def body(q, carry):
            at = half * 32 + q * 16

            def value(i):
                if i < 0:
                    row = s * 192 + half * 96 + (i + 3) * 32 + q * 16
                    return x_low[pl.ds(pl.multiple_of(row, 8), 16), :]
                if i > 7:
                    row = s * 128 + half * 64 + (i - 8) * 32 + q * 16
                    return x_high[pl.ds(pl.multiple_of(row, 8), 16), :]
                return field[pl.ds(base + at * 8 + i, 16, stride=8), :]

            def speed(k):
                return speed_x[pl.ds(pl.multiple_of(k * 64 + at, 8), 16), :]

            def emit(i, change):
                tend[pl.ds(at * 8 + i, 16, stride=8), :] = -change

            weno_line(8, value, speed, emit)
            return carry

        lax.fori_loop(0, 2, body, 0)

    def pass_y(s, half):
        base = s * FIELD + OWN

        def body(zi, carry):
            z = half * 8 + zi

            def value(i):
                if i < 0:
                    return y_low[pl.ds(pl.multiple_of((z * 3 + i + 3) * 8, 8), 8), :]
                if i > 3:
                    return y_high[pl.ds(pl.multiple_of((z * 2 + i - 4) * 8, 8), 8), :]
                return field[pl.ds(pl.multiple_of(base + z * 32 + i * 8, 8), 8), :]

            def speed(k):
                return speed_y[pl.ds(pl.multiple_of((z * 5 + k) * 8, 8), 8), :]

            def emit(i, change):
                at = pl.ds(pl.multiple_of(z * 32 + i * 8, 8), 8)
                tend[at, :] = tend[at, :] - change

            weno_line(4, value, speed, emit)
            return carry

        lax.fori_loop(0, 8, body, 0, unroll=2)

    def pass_z(s, first_level, count):
        for p in range(2):
            at = first_level * 32 + p * 16

            def value(i):
                return field[pl.ds(pl.multiple_of(s * FIELD + (i + 3) * 32 + at, 8), 16), :]

            def speed(k):
                return speed_z[pl.ds(pl.multiple_of(k * 32 + at, 8), 16), :]

            def emit(i, change):
                row = i * 32 + at
                stepped = value(i) + (tend[pl.ds(pl.multiple_of(row, 8), 16), :] - change)
                if s == 0:
                    field[pl.ds(pl.multiple_of(FIELD + OWN + row, 8), 16), :] = stepped
                else:
                    before = field[pl.ds(pl.multiple_of(OWN + row, 8), 16), :]
                    settled = 0.5 * before + 0.5 * stepped
                    for k in range(2):
                        to = (2 * p + k) * COLUMN + (first_level + i) * 8
                        levels[pl.ds(pl.multiple_of(to, 8), 8), :] = settled[8 * k : 8 * k + 8]

            weno_line(count, value, speed, emit)

    first_z, first_xy = halos_z(0), halos_xy(0, 0, 0, 2)
    start_far(first_z)
    start_far(wind_copies)
    start_near(first_z)
    start_near(wind_copies)
    start(wind_copies, (0, 1, 2, 3))
    for half in range(2):
        pack_y(0, half)
    start(first_xy, (2, 3))
    for half in range(2):
        pack_x(0, half)
    start(first_xy, (0, 1))

    loads[2].wait()
    loads[3].wait()
    rates = jnp.concatenate([rate_ref[...], rate_ref[...]], axis=1)
    counts = jnp.concatenate([steps_ref[...], steps_ref[...]], axis=1)
    tap = (lax.broadcasted_iota(jnp.int32, (32, 128), 0) == 0).astype(F32)
    fallen = jnp.zeros((32, 128), F32)
    for s in range(SUBS):
        rate = jnp.where(s < counts, rates, 0.0)
        fallen = fallen + rate * tap
        tap = tap + rate * (pltpu.roll(tap, 1, 0) - tap)
    taps[...] = tap
    rain_taps[...] = fallen

    column = jnp.where(low, 0, 64)

    def spread(v, index):
        return jnp.take_along_axis(v, index, axis=1)

    def speeds_x():
        right = 0.5 * (winds[pl.ds(8, 8), :] + winds[pl.ds(9, 8), :])
        left = jnp.broadcast_to(0.5 * (winds[pl.ds(7, 1), :] + winds[pl.ds(8, 1), :]), (8, 128))

        def body(z, carry):
            for yi in range(4):
                index = column + (16 * yi + z)
                row = z * 4 + yi
                speed_x[pl.ds(64 + row, 8, stride=64), :] = spread(right, index)
                speed_x[pl.ds(row, 1), :] = spread(left, index)[0:1, :]
            return carry

        lax.fori_loop(0, 16, body, 0, unroll=2)

    def speeds_y():
        own, before, after = (winds[pl.ds(24 + k, 8), :] for k in (8, 0, 16))
        following = jnp.where(lane < 112, pltpu.roll(own, 112, 1), pltpu.roll(after, 112, 1))
        right = 0.5 * (own + following)
        left = 0.5 * (own + pltpu.roll(before, 16, 1))

        def body(z, carry):
            first_face = jnp.where(
                low,
                spread(left, jnp.zeros_like(lane) + z),
                spread(right, jnp.zeros_like(lane) + (48 + z)),
            )
            speed_y[pl.ds(pl.multiple_of(z * 40, 8), 8), :] = first_face
            for k in range(1, 5):
                speed_y[pl.ds(pl.multiple_of(z * 40 + k * 8, 8), 8), :] = spread(
                    right, column + (16 * (k - 1) + z)
                )
            return carry

        lax.fori_loop(0, 16, body, 0, unroll=2)

    def speeds_z():
        own = winds[pl.ds(56, 8), :]
        right = 0.5 * (own + pltpu.roll(own, 127, 1))

        def body(z, carry):
            for yi in range(4):
                speed_z[pl.ds(pl.multiple_of(32 + z * 32 + yi * 8, 8), 8), :] = spread(
                    right, column + (16 * yi + z)
                )
            return carry

        lax.fori_loop(0, 15, body, 0, unroll=3)

    def speeds_bottom():
        left = 0.5 * (winds[pl.ds(56, 8), :] + pltpu.roll(winds[pl.ds(48, 8), :], 113, 1))
        for yi in range(4):
            speed_z[pl.ds(yi * 8, 8), :] = spread(left, column + 16 * yi)

    def speeds_top():
        right = 0.5 * (winds[pl.ds(56, 8), :] + pltpu.roll(winds[pl.ds(64, 8), :], 15, 1))
        for yi in range(4):
            speed_z[pl.ds(512 + yi * 8, 8), :] = spread(right, column + (16 * yi + 15))

    speeds_z()
    finish_recv(wind_copies, (0, 1))
    speeds_x()
    finish_recv(wind_copies, (2, 3))
    speeds_y()
    finish_recv(first_xy, (0, 1))
    for half in range(2):
        pass_x(0, half)
    finish_recv(first_xy, (2, 3))
    for half in range(2):
        unpack_y(0, half)
        pass_y(0, half)
    recv_near(wind_copies)
    when(even, speeds_top)
    when(odd, speeds_bottom)
    recv_near(first_z)
    pass_z(0, 3 * near_half, 13)

    second_z = halos_z(1)
    second_near = halos_xy(1, 1, near_half, 1)
    second_far = halos_xy(1, 2, far_half, 1)
    start_near(second_z)
    pack_y(1, near_half)
    start(second_near, (2, 3))
    pack_x(1, near_half)
    start(second_near, (0, 1))

    recv_far(wind_copies)
    when(even, speeds_bottom)
    when(odd, speeds_top)
    recv_far(first_z)
    pass_z(0, 13 * far_half, 3)
    start_far(second_z)
    pack_y(1, far_half)
    start(second_far, (2, 3))
    pack_x(1, far_half)
    start(second_far, (0, 1))

    def sed_copy(kind, yi):
        source, target = ((0, 16), (8, 24), (16, 32))[kind]
        return copy_of(
            levels.at[pl.ds(yi * COLUMN + source * 8, 64)],
            levels.at[pl.ds(yi * COLUMN + target * 8, 64)],
            sed_send.at[yi, kind], sed_recv.at[yi, kind], sides[4][1],
        )

    above = gz < nz - 1
    above_two = gz < nz - 2
    below = gz > 0
    hands_on = jnp.logical_and(below, above)

    def sed_start(kind):
        for yi in range(4):
            when(below, sed_copy(kind, yi).start)

    finish_recv(second_near, (0, 1))
    pass_x(1, near_half)
    finish_recv(second_near, (2, 3))
    unpack_y(1, near_half)
    pass_y(1, near_half)
    recv_near(second_z)
    pass_z(1, 8 * near_half, 8)
    when(even, lambda: sed_start(1))
    when(odd, lambda: sed_start(0))

    finish_recv(second_far, (0, 1))
    pass_x(1, far_half)
    finish_recv(second_far, (2, 3))
    unpack_y(1, far_half)
    pass_y(1, far_half)
    recv_far(second_z)
    pass_z(1, 8 * far_half, 8)
    when(even, lambda: sed_start(0))
    when(odd, lambda: sed_start(1))

    for yi in range(4):
        when(above, sed_copy(0, yi).wait_recv)
        when(hands_on, sed_copy(2, yi).start)

    def rain_copy(step):
        return copy_of(
            rain, rain, rain_send.at[step - 1], rain_recv.at[step - 1],
            {"gz": lax.rem(gz + step, nz)},
        )

    lowest = gz == 0
    sends_far = jnp.logical_and(even, above_two)
    follows = jnp.logical_and(even, gz > 0)

    def rain_make():
        def body(yi, carry):
            total = jnp.zeros((8, 128), F32)
            for m in range(SUBS):
                at = pl.ds(pl.multiple_of(yi * COLUMN + m * 8, 8), 8)
                total = total + rain_taps[pl.ds(m, 1), :] * levels[at, :]
            rain[pl.ds(pl.multiple_of(yi * 8, 8), 8), :] = total
            return carry

        lax.fori_loop(0, 4, body, 0)

    def rain_pass():
        rain_copy(1).start()
        when(sends_far, rain_copy(2).start)

    def rain_first():
        rain_make()
        rain_pass()

    def rain_forward():
        rain_copy(2).wait_recv()
        rain_pass()

    when(lowest, rain_first)

    loads[4].wait()
    loads[5].wait()

    def settle(u, group):
        def body(k2, carry):
            base = pl.multiple_of((2 * u + k2) * COLUMN + group * 64, 64)
            sums = [None] * 8
            for j in range(8 + SUBS):
                v = levels[pl.ds(base + j * 8, 8), :]
                for k in range(8):
                    if 0 <= j - k <= SUBS:
                        term = taps[pl.ds(j - k, 1), :] * v
                        sums[k] = term if sums[k] is None else sums[k] + term
            for k in range(8):
                stage[pl.ds(pl.multiple_of(k2 * 64 + k * 8, 8), 8), :] = sums[k]
            return carry

        lax.fori_loop(0, 2, body, 0)

    def breakup(u, group):
        block = jnp.concatenate(
            [stage[pl.ds(k2 * 64 + x, 8, stride=8), :] for k2 in range(2) for x in range(8)], axis=0
        ).T
        for h in range(2):
            cells[:, 128 * h : 128 * h + 128] = block[64 * h : 64 * h + 64]
        small = cells[...].astype(BF16)
        rounded[...] = small.astype(F32)

        def body(i, total):
            wide = rounded[...]
            terms = [rounded[pl.ds(i * 4 + k, 1), :] * wide for k in range(4)]
            block = jnp.concatenate(terms, axis=0).astype(BF16)
            part = gains[:, pl.ds(pl.multiple_of(i * 256, 256), 256)]
            return total + jnp.dot(part, block, preferred_element_type=F32)

        loss = lax.dot_general(
            collide_ref[...], small, (((0,), (0,)), ((), ())), preferred_element_type=F32
        )
        gained = lax.fori_loop(0, 16, body, jnp.zeros((64, 256), F32), unroll=4)
        settled = cells[...]
        result = settled + gained - settled * loss
        for h in range(2):
            back = result[:, 128 * h : 128 * h + 128].T
            for k2 in range(2):
                out_ref[:, 4 * h + 2 * u + k2, 8 * group : 8 * group + 8, :] = back[
                    64 * k2 : 64 * k2 + 64
                ].reshape(8, 8, 64)

    for u in range(2):
        for yi in (2 * u, 2 * u + 1):
            when(above, sed_copy(1, yi).wait_recv)
        settle(u, 0)
        breakup(u, 0)
    when(follows, rain_forward)
    for u in range(2):
        for yi in (2 * u, 2 * u + 1):
            when(above_two, sed_copy(2, yi).wait_recv)
        settle(u, 1)
        breakup(u, 1)

    when(odd, rain_copy(1).wait_recv)
    mine = rain[pl.ds(pl.multiple_of(lax.rem(gz, 4) * 8, 8), 8), :]
    upper = (jnp.zeros((8, 128), jnp.int32) + gz) >= 4
    rain_ref[:, 0, :] = jnp.where(upper, turn(mine), mine)[:, :64]

    when(even, rain_copy(1).wait_send)
    when(sends_far, rain_copy(2).wait_send)
    for yi in range(4):
        when(below, sed_copy(0, yi).wait_send)
        when(below, sed_copy(1, yi).wait_send)
        when(hands_on, sed_copy(2, yi).wait_send)
    finish_send(wind_copies)
    for copies in (first_z, first_xy, second_z, second_near, second_far):
        finish_send(copies)


def per_device(sizes, bin_mass, courant, sub_courant, fall_steps, frag_gain, collide):
    vmem, dma = pltpu.VMEM, pltpu.SemaphoreType.DMA
    out, rain = pl.pallas_call(
        functools.partial(kernel, *sizes),
        out_shape=(
            jax.ShapeDtypeStruct((8, 8, 16, 64), F32),
            jax.ShapeDtypeStruct((8, 1, 64), F32),
        ),
        in_specs=[pl.BlockSpec(memory_space=pl.ANY)] * 6,
        out_specs=(pl.BlockSpec(memory_space=vmem), pl.BlockSpec(memory_space=vmem)),
        scratch_shapes=[
            vmem((1024, 64), F32),
            vmem((3, 8, 8, 16), F32),
            vmem((1, 64), F32),
            vmem((1, 64), jnp.int32),
            vmem((64, 4096), BF16),
            vmem((64, 64), BF16),
            vmem((2 * FIELD, 128), F32),
            vmem((512, 128), F32),
            vmem((384, 128), F32),
            vmem((256, 128), F32),
            vmem((640, 128), F32),
            vmem((384, 128), F32),
            vmem((256, 128), F32),
            vmem((640, 128), F32),
            vmem((640, 128), F32),
            vmem((72, 128), F32),
            vmem((9 * 64, 128), F32),
            vmem((16 * 40, 128), F32),
            vmem((17 * 32, 128), F32),
            vmem((32, 128), F32),
            vmem((32, 128), F32),
            vmem((4 * COLUMN, 128), F32),
            vmem((128, 128), F32),
            vmem((64, 256), F32),
            vmem((64, 256), F32),
            vmem((32, 128), F32),
            dma((6,)),
            dma((3, 6)),
            dma((3, 6)),
            dma((6,)),
            dma((6,)),
            dma((4, 3)),
            dma((4, 3)),
            dma((2,)),
            dma((2,)),
        ],
        compiler_params=pltpu.CompilerParams(
            collective_id=0, has_side_effects=True, vmem_limit_bytes=60 << 20
        ),
    )(
        bin_mass.reshape(1024, 64),
        courant,
        sub_courant.reshape(1, 64),
        fall_steps.reshape(1, 64),
        frag_gain.T,
        collide,
    )
    return out, rain


def solution(mesh):
    in_specs = (P("gx", "gy", "gz", None), P(None, "gx", "gy", "gz"), P(), P(), P(), P())
    out_specs = (P("gx", "gy", "gz", None), P("gx", ("gy", "gz"), None))
    sizes = tuple(mesh.shape[a] for a in ("gx", "gy", "gz"))
    return jax.shard_map(
        functools.partial(per_device, sizes),
        mesh=mesh,
        in_specs=in_specs,
        out_specs=out_specs,
        check_vma=False,
    )
```

```python
import functools

import jax
import jax.numpy as jnp
from jax import lax
from jax.experimental import pallas as pl
from jax.experimental.pallas import tpu as pltpu
from jax.sharding import PartitionSpec as P

MESH = pl.DeviceIdType.MESH
SUBS = 24
EPS4 = 4e-6
F32 = jnp.float32
BF16 = jnp.bfloat16

OWN = 3 * 32
TOP = 19 * 32
FIELD = 21 * 32
COLUMN = 40 * 8


def weno_line(count, value, speed, emit):
    f_a, f_b, f_c, f_d = value(-3), value(-2), value(-1), value(0)
    d_prev, d_here, d_next = f_b - f_a, f_c - f_b, f_d - f_c
    half_here, half_next = 0.5 * f_c, 0.5 * f_d

    def smooth(e):
        return (13.0 / 3.0) * (e * e) + EPS4

    e_low, e_mid = d_here - d_prev, d_next - d_here
    q_low, q_mid = smooth(e_low), smooth(e_mid)
    t_low = e_mid - e_low
    f_last = f_d
    flux_prev = None
    for face in range(count + 1):
        f_new = value(face + 1)
        d_new = f_new - f_last
        e_high = d_new - d_next
        q_high = smooth(e_high)
        t_high = e_high - e_mid
        g_low = e_low + 2.0 * d_here
        g_mid = d_here + d_next
        g_high = e_high - 2.0 * d_next
        b_low = q_low + g_low * g_low
        b_mid = q_mid + g_mid * g_mid
        b_high = q_high + g_high * g_high
        w_low = b_mid * b_high
        w_mid = b_low * b_high
        w_high = b_low * b_mid
        w_low = w_low * w_low
        w_mid = w_mid * w_mid
        w_high = 0.5 * (w_high * w_high)
        num = w_low * ((1.0 / 3.0) * t_low) + w_high * t_high
        den = w_low + 6.0 * (w_mid + w_high)
        central = (half_here + half_next) - (1.0 / 6.0) * e_mid
        flux = speed(face) * (central - num * pl.reciprocal(den, approx=True))
        if face:
            emit(face - 1, flux - flux_prev)
        flux_prev = flux
        f_last = f_new
        half_here, half_next = half_next, 0.5 * f_new
        d_here, d_next = d_next, d_new
        e_low, e_mid = e_mid, e_high
        q_low, q_mid = q_mid, q_high
        t_low = t_high


def kernel(
    nx, ny, nz,
    mass_hbm, courant_hbm, rate_hbm, steps_hbm, gain_hbm, collide_hbm,
    out_ref, rain_ref,
    raw, courant_ref, rate_ref, steps_ref, gains, collide_ref, field, tend, x_low, x_high, x_out, y_low, y_high, y_out, y_in, winds,
    speed_x, speed_y, speed_z, taps, rain_taps, levels, stage, cells, rounded, rain, done, rain_done,
    load_sem, halo_send, halo_recv, wind_send, wind_recv, sed_send, sed_recv, rain_send, rain_recv,
    store_sem,
):
    gx, gy, gz = lax.axis_index("gx"), lax.axis_index("gy"), lax.axis_index("gz")
    parity = lax.rem(gz, 2)
    odd = parity == 1
    even = parity == 0
    near_half, far_half = 1 - parity, parity

    def when(cond, fn):
        pl.when(cond)(fn)

    sides = [
        (gx > 0, {"gx": lax.rem(gx + nx - 1, nx)}),
        (gx < nx - 1, {"gx": lax.rem(gx + 1, nx)}),
        (gy > 0, {"gy": lax.rem(gy + ny - 1, ny)}),
        (gy < ny - 1, {"gy": lax.rem(gy + 1, ny)}),
        (gz > 0, {"gz": lax.rem(gz + nz - 1, nz)}),
        (gz < nz - 1, {"gz": lax.rem(gz + 1, nz)}),
    ]

    barrier = pltpu.get_barrier_semaphore()
    for there, where in sides:
        when(
            there,
            lambda where=where: pl.semaphore_signal(
                barrier, inc=1, device_id=where, device_id_type=MESH
            ),
        )
    loads = [
        pltpu.make_async_copy(source, target, load_sem.at[k])
        for k, (source, target) in enumerate(
            (
                (mass_hbm, raw),
                (courant_hbm, courant_ref),
                (rate_hbm, rate_ref),
                (steps_hbm, steps_ref),
                (gain_hbm, gains),
                (collide_hbm, collide_ref),
            )
        )
    ]
    for load in loads:
        load.start()

    lane = lax.broadcasted_iota(jnp.int32, (8, 128), 1)
    low = lane < 64

    def turn(v):
        return pltpu.roll(v, 64, 1)

    def fill(ref, start, rows):
        ref[pl.ds(start, rows), :] = jnp.zeros((rows, 128), F32)

    def no_x_low():
        fill(x_low, 0, 384)
        fill(winds, 0, 8)

    def no_x_high():
        fill(x_high, 0, 256)
        fill(winds, 16, 8)

    def no_y_low():
        fill(y_in, 0, 384)
        fill(winds, 24, 8)

    def no_y_high():
        fill(y_in, 384, 256)
        fill(winds, 40, 8)

    def no_z_low():
        fill(field, 0, OWN)
        fill(field, FIELD, OWN)
        fill(winds, 48, 8)

    def no_z_high():
        fill(field, TOP, 64)
        fill(field, FIELD + TOP, 64)
        fill(winds, 64, 8)
        for yi in range(4):
            fill(levels, yi * COLUMN + 128, 128)

    for (there, _), fn in zip(
        sides, (no_x_low, no_x_high, no_y_low, no_y_high, no_z_low, no_z_high)
    ):
        when(jnp.logical_not(there), fn)
    def none_above():
        for yi in range(4):
            fill(levels, yi * COLUMN + 256, 64)

    when(gz >= nz - 2, none_above)

    loads[0].wait()

    def pack(z, carry):
        for yi in range(4):
            lo = raw[pl.ds(16 * yi + z, 8, stride=128), :]
            hi = raw[pl.ds(16 * (yi + 4) + z, 8, stride=128), :]
            field[pl.ds(pl.multiple_of(OWN + z * 32 + yi * 8, 8), 8), :] = jnp.concatenate(
                [lo, hi], axis=1
            )
        return carry

    lax.fori_loop(0, 16, pack, 0, unroll=2)

    loads[1].wait()
    for d in range(3):
        for y in range(8):
            winds[pl.ds(d * 24 + 8, 8), pl.ds(16 * y, 16)] = courant_ref[d, :, y, :]

    waits = jnp.int32(0)
    for there, _ in sides:
        waits = waits + there.astype(jnp.int32)
    pl.semaphore_wait(barrier, waits)

    def copy_of(src, dst, send, recv, where):
        return pltpu.make_async_remote_copy(
            src_ref=src, dst_ref=dst, send_sem=send, recv_sem=recv,
            device_id=where, device_id_type=MESH,
        )

    def halo(s, slot, to, src, dst):
        return (
            to,
            to ^ 1,
            copy_of(src, dst, halo_send.at[slot, to], halo_recv.at[slot, to], sides[to][1]),
        )

    def halos_xy(s, slot, half, halves):
        def at(start, rows):
            return pl.ds(pl.multiple_of(start + half * rows, 8), rows * halves)

        return [
            halo(s, slot, 0, x_out.at[at(s * 320 + 192, 64)], x_high.at[at(s * 128, 64)]),
            halo(s, slot, 1, x_out.at[at(s * 320, 96)], x_low.at[at(s * 192, 96)]),
            halo(s, slot, 2, y_out.at[at(s * 320 + 192, 64)], y_in.at[at(384 + s * 128, 64)]),
            halo(s, slot, 3, y_out.at[at(s * 320, 96)], y_in.at[at(s * 192, 96)]),
        ]

    def halos_z(s):
        base = s * FIELD
        return [
            halo(s, s, 4, field.at[pl.ds(base + OWN, 64)], field.at[pl.ds(base + TOP, 64)]),
            halo(s, s, 5, field.at[pl.ds(base + TOP - 96, 96)], field.at[pl.ds(base, 96)]),
        ]

    wind_copies = []
    for d in range(3):
        own = winds.at[pl.ds(d * 24 + 8, 8)]
        for to in (2 * d, 2 * d + 1):
            dst = winds.at[pl.ds(d * 24 + (16 if to == 2 * d else 0), 8)]
            wind_copies.append(
                (to, to ^ 1, copy_of(own, dst, wind_send.at[to], wind_recv.at[to], sides[to][1]))
            )

    def start(copies, only):
        for to, _, copy in copies:
            if to in only:
                when(sides[to][0], copy.start)

    def finish_recv(copies, only):
        for to, source, copy in copies:
            if source in only:
                when(sides[source][0], copy.wait_recv)

    def finish_send(copies):
        for to, _, copy in copies:
            when(sides[to][0], copy.wait_send)

    def by_parity(even_side, fn):
        when(even, lambda: fn((even_side,)))
        when(odd, lambda: fn((9 - even_side,)))

    def start_near(copies):
        by_parity(5, lambda only: start(copies, only))

    def start_far(copies):
        by_parity(4, lambda only: start(copies, only))

    def recv_near(copies):
        by_parity(5, lambda only: finish_recv(copies, only))

    def recv_far(copies):
        by_parity(4, lambda only: finish_recv(copies, only))

    def pack_x(s, half):
        base = s * FIELD + OWN + half * 256
        for k in range(3):
            x_out[pl.ds(pl.multiple_of(s * 320 + half * 96 + k * 32, 8), 32), :] = field[
                pl.ds(base + 5 + k, 32, stride=8), :
            ]
        for k in range(2):
            x_out[pl.ds(pl.multiple_of(s * 320 + 192 + half * 64 + k * 32, 8), 32), :] = field[
                pl.ds(base + k, 32, stride=8), :
            ]

    def pack_y(s, half):
        base = s * FIELD + OWN + half * 256
        for zi in range(4):
            here = base + zi * 32
            for k in range(3):
                lo = field[pl.ds(pl.multiple_of(here + (k + 1) * 8, 8), 8), :]
                hi = field[pl.ds(pl.multiple_of(here + 128 + (k + 1) * 8, 8), 8), :]
                at = s * 320 + half * 96 + (zi * 3 + k) * 8
                y_out[pl.ds(pl.multiple_of(at, 8), 8), :] = jnp.where(low, turn(lo), hi)
            for k in range(2):
                lo = field[pl.ds(pl.multiple_of(here + k * 8, 8), 8), :]
                hi = field[pl.ds(pl.multiple_of(here + 128 + k * 8, 8), 8), :]
                at = s * 320 + 192 + half * 64 + (zi * 2 + k) * 8
                y_out[pl.ds(pl.multiple_of(at, 8), 8), :] = jnp.where(low, lo, turn(hi))

    def unpack_y(s, half):
        base = s * FIELD + OWN + half * 256
        for zi in range(4):
            here = base + zi * 32
            for k in range(3):
                at = half * 96 + (zi * 3 + k) * 8
                got = y_in[pl.ds(pl.multiple_of(s * 192 + at, 8), 8), :]
                own_a = turn(field[pl.ds(pl.multiple_of(here + (k + 1) * 8, 8), 8), :])
                own_b = turn(field[pl.ds(pl.multiple_of(here + 128 + (k + 1) * 8, 8), 8), :])
                at = half * 192 + (zi * 3 + k) * 8
                y_low[pl.ds(pl.multiple_of(at, 8), 8), :] = jnp.where(low, got, own_a)
                y_low[pl.ds(pl.multiple_of(at + 96, 8), 8), :] = jnp.where(low, turn(got), own_b)
            for k in range(2):
                at = 384 + s * 128 + half * 64 + (zi * 2 + k) * 8
                got = y_in[pl.ds(pl.multiple_of(at, 8), 8), :]
                own_a = turn(field[pl.ds(pl.multiple_of(here + k * 8, 8), 8), :])
                own_b = turn(field[pl.ds(pl.multiple_of(here + 128 + k * 8, 8), 8), :])
                at = half * 128 + (zi * 2 + k) * 8
                y_high[pl.ds(pl.multiple_of(at, 8), 8), :] = jnp.where(low, own_a, turn(got))
                y_high[pl.ds(pl.multiple_of(at + 64, 8), 8), :] = jnp.where(low, own_b, got)

    def pass_x(s, half, fresh):
        base = s * FIELD + OWN

        def body(q, carry):
            at = half * 32 + q * 16

            def value(i):
                if i < 0:
                    row = s * 192 + half * 96 + (i + 3) * 32 + q * 16
                    return x_low[pl.ds(pl.multiple_of(row, 8), 16), :]
                if i > 7:
                    row = s * 128 + half * 64 + (i - 8) * 32 + q * 16
                    return x_high[pl.ds(pl.multiple_of(row, 8), 16), :]
                return field[pl.ds(base + at * 8 + i, 16, stride=8), :]

            def speed(k):
                return speed_x[pl.ds(pl.multiple_of(k * 64 + at, 8), 16), :]

            def emit(i, change):
                to = pl.ds(at * 8 + i, 16, stride=8)
                tend[to, :] = -change if fresh else tend[to, :] - change

            weno_line(8, value, speed, emit)
            return carry

        lax.fori_loop(0, 2, body, 0)

    def pass_y(s, first_level, count, last):
        base = s * FIELD + OWN

        def body(k, carry):
            z = first_level + k

            def value(i):
                if i < 0:
                    return y_low[pl.ds(pl.multiple_of((z * 3 + i + 3) * 8, 8), 8), :]
                if i > 3:
                    return y_high[pl.ds(pl.multiple_of((z * 2 + i - 4) * 8, 8), 8), :]
                return field[pl.ds(pl.multiple_of(base + z * 32 + i * 8, 8), 8), :]

            def speed(k):
                return speed_y[pl.ds(pl.multiple_of((z * 5 + k) * 8, 8), 8), :]

            def emit(i, change):
                row = z * 32 + i * 8
                at = pl.ds(pl.multiple_of(row, 8), 8)
                total = tend[at, :] - change
                if not last:
                    tend[at, :] = total
                    return
                stepped = value(i) + total
                if s == 0:
                    field[pl.ds(pl.multiple_of(FIELD + OWN + row, 8), 8), :] = stepped
                else:
                    before = field[pl.ds(pl.multiple_of(OWN + row, 8), 8), :]
                    to = pl.ds(pl.multiple_of(i * COLUMN + z * 8, 8), 8)
                    levels[to, :] = 0.5 * before + 0.5 * stepped

            weno_line(4, value, speed, emit)
            return carry

        unroll = 2 if count % 2 == 0 else 1
        lax.fori_loop(0, count, body, 0, unroll=unroll)

    def pass_z(s, first_level, count, last):
        for p in range(2):
            at = first_level * 32 + p * 16

            def value(i):
                return field[pl.ds(pl.multiple_of(s * FIELD + (i + 3) * 32 + at, 8), 16), :]

            def speed(k):
                return speed_z[pl.ds(pl.multiple_of(k * 32 + at, 8), 16), :]

            def emit(i, change):
                row = i * 32 + at
                if not last:
                    tend[pl.ds(pl.multiple_of(row, 8), 16), :] = -change
                    return
                stepped = value(i) + (tend[pl.ds(pl.multiple_of(row, 8), 16), :] - change)
                if s == 0:
                    field[pl.ds(pl.multiple_of(FIELD + OWN + row, 8), 16), :] = stepped
                else:
                    before = field[pl.ds(pl.multiple_of(OWN + row, 8), 16), :]
                    settled = 0.5 * before + 0.5 * stepped
                    for k in range(2):
                        to = (2 * p + k) * COLUMN + (first_level + i) * 8
                        levels[pl.ds(pl.multiple_of(to, 8), 8), :] = settled[8 * k : 8 * k + 8]

            weno_line(count, value, speed, emit)

    first_z, first_xy = halos_z(0), halos_xy(0, 0, 0, 2)
    start_far(first_z)
    start_far(wind_copies)
    start_near(first_z)
    start_near(wind_copies)
    start(wind_copies, (0, 1, 2, 3))
    for half in range(2):
        pack_y(0, half)
    start(first_xy, (2, 3))
    for half in range(2):
        pack_x(0, half)
    start(first_xy, (0, 1))

    loads[2].wait()
    loads[3].wait()
    rates = jnp.concatenate([rate_ref[...], rate_ref[...]], axis=1)
    counts = jnp.concatenate([steps_ref[...], steps_ref[...]], axis=1)
    tap = (lax.broadcasted_iota(jnp.int32, (32, 128), 0) == 0).astype(F32)
    fallen = jnp.zeros((32, 128), F32)
    for s in range(SUBS):
        rate = jnp.where(s < counts, rates, 0.0)
        fallen = fallen + rate * tap
        tap = tap + rate * (pltpu.roll(tap, 1, 0) - tap)
    taps[...] = tap
    rain_taps[...] = fallen

    column = jnp.where(low, 0, 64)

    def spread(v, index):
        return jnp.take_along_axis(v, index, axis=1)

    def speeds_x():
        right = 0.5 * (winds[pl.ds(8, 8), :] + winds[pl.ds(9, 8), :])
        left = jnp.broadcast_to(0.5 * (winds[pl.ds(7, 1), :] + winds[pl.ds(8, 1), :]), (8, 128))

        def body(z, carry):
            for yi in range(4):
                index = column + (16 * yi + z)
                row = z * 4 + yi
                speed_x[pl.ds(64 + row, 8, stride=64), :] = spread(right, index)
                speed_x[pl.ds(row, 1), :] = spread(left, index)[0:1, :]
            return carry

        lax.fori_loop(0, 16, body, 0, unroll=2)

    def speeds_y():
        own, before, after = (winds[pl.ds(24 + k, 8), :] for k in (8, 0, 16))
        following = jnp.where(lane < 112, pltpu.roll(own, 112, 1), pltpu.roll(after, 112, 1))
        right = 0.5 * (own + following)
        left = 0.5 * (own + pltpu.roll(before, 16, 1))

        def body(z, carry):
            first_face = jnp.where(
                low,
                spread(left, jnp.zeros_like(lane) + z),
                spread(right, jnp.zeros_like(lane) + (48 + z)),
            )
            speed_y[pl.ds(pl.multiple_of(z * 40, 8), 8), :] = first_face
            for k in range(1, 5):
                speed_y[pl.ds(pl.multiple_of(z * 40 + k * 8, 8), 8), :] = spread(
                    right, column + (16 * (k - 1) + z)
                )
            return carry

        lax.fori_loop(0, 16, body, 0, unroll=2)

    def speeds_z():
        own = winds[pl.ds(56, 8), :]
        right = 0.5 * (own + pltpu.roll(own, 127, 1))

        def body(z, carry):
            for yi in range(4):
                speed_z[pl.ds(pl.multiple_of(32 + z * 32 + yi * 8, 8), 8), :] = spread(
                    right, column + (16 * yi + z)
                )
            return carry

        lax.fori_loop(0, 15, body, 0, unroll=3)

    def speeds_bottom():
        left = 0.5 * (winds[pl.ds(56, 8), :] + pltpu.roll(winds[pl.ds(48, 8), :], 113, 1))
        for yi in range(4):
            speed_z[pl.ds(yi * 8, 8), :] = spread(left, column + 16 * yi)

    def speeds_top():
        right = 0.5 * (winds[pl.ds(56, 8), :] + pltpu.roll(winds[pl.ds(64, 8), :], 15, 1))
        for yi in range(4):
            speed_z[pl.ds(512 + yi * 8, 8), :] = spread(right, column + (16 * yi + 15))

    speeds_z()
    finish_recv(wind_copies, (0, 1))
    speeds_x()
    finish_recv(wind_copies, (2, 3))
    speeds_y()
    recv_near(wind_copies)
    when(even, speeds_top)
    when(odd, speeds_bottom)
    finish_recv(first_xy, (0, 1))
    for half in range(2):
        pass_x(0, half, True)
    finish_recv(first_xy, (2, 3))
    for half in range(2):
        unpack_y(0, half)
    pass_y(0, 0, 16, False)
    recv_near(first_z)
    pass_z(0, 3 * near_half, 13, True)

    second_z = halos_z(1)
    second_near = halos_xy(1, 1, near_half, 1)
    second_far = halos_xy(1, 2, far_half, 1)
    start_near(second_z)
    pack_y(1, near_half)
    start(second_near, (2, 3))
    pack_x(1, near_half)
    start(second_near, (0, 1))

    recv_far(wind_copies)
    when(even, speeds_bottom)
    when(odd, speeds_top)
    recv_far(first_z)
    pass_z(0, 13 * far_half, 3, True)
    start_far(second_z)
    pack_y(1, far_half)
    start(second_far, (2, 3))
    pack_x(1, far_half)
    start(second_far, (0, 1))

    def sed_copy(kind, yi):
        source, target = ((0, 16), (8, 24), (16, 32))[kind]
        return copy_of(
            levels.at[pl.ds(pl.multiple_of(yi * COLUMN + source * 8, 64), 64)],
            levels.at[pl.ds(pl.multiple_of(yi * COLUMN + target * 8, 64), 64)],
            sed_send.at[yi, kind], sed_recv.at[yi, kind], sides[4][1],
        )

    above = gz < nz - 1
    above_two = gz < nz - 2
    below = gz > 0
    hands_on = jnp.logical_and(below, above)

    def sed_start(kind):
        for yi in range(4):
            when(below, sed_copy(kind, yi).start)

    finish_recv(second_near, (0, 1))
    pass_x(1, near_half, True)
    finish_recv(second_near, (2, 3))
    unpack_y(1, near_half)
    pass_y(1, 8 * near_half, 8, False)
    recv_near(second_z)
    pass_z(1, 8 * near_half, 8, True)
    when(even, lambda: sed_start(1))
    when(odd, lambda: sed_start(0))

    finish_recv(second_far, (0, 1))
    pass_x(1, far_half, True)
    finish_recv(second_far, (2, 3))
    unpack_y(1, far_half)
    pass_y(1, 8 * far_half, 8, False)
    recv_far(second_z)
    pass_z(1, 8 * far_half, 8, True)

    def hand_on(u):
        for k in range(2):
            when(above, sed_copy(0, 2 * u + k).wait_recv)
            when(hands_on, sed_copy(2, 2 * u + k).start)

    def far_even():
        for yi in range(4):
            when(below, sed_copy(0, yi).start)
        for u in range(2):
            hand_on(u)

    when(even, far_even)
    when(odd, lambda: sed_start(1))

    def rain_copy(step):
        return copy_of(
            rain, rain, rain_send.at[step - 1], rain_recv.at[step - 1],
            {"gz": lax.rem(gz + step, nz)},
        )

    lowest = gz == 0
    sends_far = jnp.logical_and(even, above_two)
    follows = jnp.logical_and(even, gz > 0)

    def rain_make():
        def body(yi, carry):
            total = jnp.zeros((8, 128), F32)
            for m in range(SUBS):
                at = pl.ds(pl.multiple_of(yi * COLUMN + m * 8, 8), 8)
                total = total + rain_taps[pl.ds(m, 1), :] * levels[at, :]
            rain[pl.ds(pl.multiple_of(yi * 8, 8), 8), :] = total
            return carry

        lax.fori_loop(0, 4, body, 0)

    def rain_pass():
        rain_copy(1).start()
        when(sends_far, rain_copy(2).start)

    def rain_first():
        rain_make()
        rain_pass()

    def rain_forward():
        rain_copy(2).wait_recv()
        rain_pass()

    when(lowest, rain_first)

    loads[4].wait()
    loads[5].wait()

    def settle(u, group):
        def body(k2, carry):
            base = pl.multiple_of((2 * u + k2) * COLUMN + group * 64, 64)
            sums = [None] * 8
            for j in range(8 + SUBS):
                v = levels[pl.ds(base + j * 8, 8), :]
                for k in range(8):
                    if 0 <= j - k <= SUBS:
                        term = taps[pl.ds(j - k, 1), :] * v
                        sums[k] = term if sums[k] is None else sums[k] + term
            for k in range(8):
                stage[pl.ds(pl.multiple_of(k2 * 64 + k * 8, 8), 8), :] = sums[k]
            return carry

        lax.fori_loop(0, 2, body, 0)

    def breakup(u, group):
        block = jnp.concatenate(
            [stage[pl.ds(k2 * 64 + x, 8, stride=8), :] for k2 in range(2) for x in range(8)], axis=0
        ).T
        for h in range(2):
            cells[:, 128 * h : 128 * h + 128] = block[64 * h : 64 * h + 64]
        small = cells[...].astype(BF16)
        rounded[...] = small.astype(F32)

        def body(i, total):
            wide = rounded[...]
            terms = [rounded[pl.ds(i * 4 + k, 1), :] * wide for k in range(4)]
            block = jnp.concatenate(terms, axis=0).astype(BF16)
            part = gains[:, pl.ds(pl.multiple_of(i * 256, 256), 256)]
            return total + jnp.dot(part, block, preferred_element_type=F32)

        loss = lax.dot_general(
            collide_ref[...], small, (((0,), (0,)), ((), ())), preferred_element_type=F32
        )
        gained = lax.fori_loop(0, 16, body, jnp.zeros((64, 256), F32), unroll=4)
        settled = cells[...]
        result = settled + gained - settled * loss
        for h in range(2):
            back = result[:, 128 * h : 128 * h + 128].T
            for k2 in range(2):
                done[
                    :, pl.ds(4 * h + 2 * u + k2, 1), pl.ds(pl.multiple_of(8 * group, 8), 8), :
                ] = back[64 * k2 : 64 * k2 + 64].reshape(8, 1, 8, 64)

    def unit_of(t):
        outer, inner = t // 2, t % 2
        return parity * outer + (1 - parity) * inner, parity * inner + (1 - parity) * outer

    def store(t, h):
        u, group = unit_of(t)
        where = (
            slice(None),
            pl.ds(4 * h + 2 * u, 2),
            pl.ds(pl.multiple_of(8 * group, 8), 8),
            slice(None),
        )
        return pltpu.make_async_copy(done.at[where], out_ref.at[where], store_sem.at[t, h])

    def both(a, b):
        return jnp.logical_and(a, b)

    for t in range(4):
        u, group = unit_of(t)
        if t % 2 == 0:
            when(odd, lambda u=u: hand_on(u))
        for k in range(2):
            when(both(group == 0, above), sed_copy(1, 2 * u + k).wait_recv)
        if t == 2:
            when(follows, rain_forward)
        for k in range(2):
            when(both(group == 1, above_two), sed_copy(2, 2 * u + k).wait_recv)
        settle(u, group)
        breakup(u, group)
        for h in range(2):
            store(t, h).start()

    when(odd, rain_copy(1).wait_recv)
    mine = rain[pl.ds(pl.multiple_of(lax.rem(gz, 4) * 8, 8), 8), :]
    upper = (jnp.zeros((8, 128), jnp.int32) + gz) >= 4
    rain_done[:, 0, :] = jnp.where(upper, turn(mine), mine)[:, :64]
    rain_store = pltpu.make_async_copy(rain_done, rain_ref, load_sem.at[0])
    rain_store.start()

    when(even, rain_copy(1).wait_send)
    when(sends_far, rain_copy(2).wait_send)
    for yi in range(4):
        when(below, sed_copy(0, yi).wait_send)
        when(below, sed_copy(1, yi).wait_send)
        when(hands_on, sed_copy(2, yi).wait_send)
    finish_send(wind_copies)
    for t in range(4):
        for h in range(2):
            store(t, h).wait()
    rain_store.wait()
    for copies in (first_z, first_xy, second_z, second_near, second_far):
        finish_send(copies)


def hand_over(mass_ref, fall_ref, out_ref, rain_ref, mass, fall, sem):
    reads = [pltpu.make_async_copy(fall_ref, fall, sem.at[0, 8])]
    writes = [pltpu.make_async_copy(fall, rain_ref, sem.at[1, 8])]
    for k in range(8):
        reads.append(pltpu.make_async_copy(mass_ref.at[k], mass.at[k], sem.at[0, k]))
        writes.append(pltpu.make_async_copy(mass.at[k], out_ref.at[k], sem.at[1, k]))
    for copy in reads:
        copy.start()
    for read, write in zip(reads, writes):
        read.wait()
        write.start()
    for copy in writes:
        copy.wait()


def per_device(sizes, bin_mass, courant, sub_courant, fall_steps, frag_gain, collide):
    vmem, dma = pltpu.VMEM, pltpu.SemaphoreType.DMA
    out, rain = pl.pallas_call(
        functools.partial(kernel, *sizes),
        out_shape=(
            jax.ShapeDtypeStruct((8, 8, 16, 64), F32),
            jax.ShapeDtypeStruct((8, 1, 64), F32),
        ),
        in_specs=[pl.BlockSpec(memory_space=pl.ANY)] * 6,
        out_specs=(pl.BlockSpec(memory_space=pl.ANY), pl.BlockSpec(memory_space=pl.ANY)),
        scratch_shapes=[
            vmem((1024, 64), F32),
            vmem((3, 8, 8, 16), F32),
            vmem((1, 64), F32),
            vmem((1, 64), jnp.int32),
            vmem((64, 4096), BF16),
            vmem((64, 64), BF16),
            vmem((2 * FIELD, 128), F32),
            vmem((512, 128), F32),
            vmem((384, 128), F32),
            vmem((256, 128), F32),
            vmem((640, 128), F32),
            vmem((384, 128), F32),
            vmem((256, 128), F32),
            vmem((640, 128), F32),
            vmem((640, 128), F32),
            vmem((72, 128), F32),
            vmem((9 * 64, 128), F32),
            vmem((16 * 40, 128), F32),
            vmem((17 * 32, 128), F32),
            vmem((32, 128), F32),
            vmem((32, 128), F32),
            vmem((4 * COLUMN, 128), F32),
            vmem((128, 128), F32),
            vmem((64, 256), F32),
            vmem((64, 256), F32),
            vmem((32, 128), F32),
            vmem((8, 8, 16, 64), F32),
            vmem((8, 1, 64), F32),
            dma((6,)),
            dma((3, 6)),
            dma((3, 6)),
            dma((6,)),
            dma((6,)),
            dma((4, 3)),
            dma((4, 3)),
            dma((2,)),
            dma((2,)),
            dma((4, 2)),
        ],
        compiler_params=pltpu.CompilerParams(
            collective_id=0, has_side_effects=True, vmem_limit_bytes=60 << 20
        ),
    )(
        bin_mass.reshape(1024, 64),
        courant,
        sub_courant.reshape(1, 64),
        fall_steps.reshape(1, 64),
        frag_gain.T,
        collide,
    )
    return pl.pallas_call(
        hand_over,
        out_shape=(
            jax.ShapeDtypeStruct((8, 8, 16, 64), F32),
            jax.ShapeDtypeStruct((8, 1, 64), F32),
        ),
        in_specs=[pl.BlockSpec(memory_space=pl.ANY)] * 2,
        out_specs=(pl.BlockSpec(memory_space=pl.ANY), pl.BlockSpec(memory_space=pl.ANY)),
        scratch_shapes=[vmem((8, 8, 16, 64), F32), vmem((8, 1, 64), F32), dma((2, 9))],
        compiler_params=pltpu.CompilerParams(vmem_limit_bytes=60 << 20),
    )(out, rain)


def solution(mesh):
    in_specs = (P("gx", "gy", "gz", None), P(None, "gx", "gy", "gz"), P(), P(), P(), P())
    out_specs = (P("gx", "gy", "gz", None), P("gx", ("gy", "gz"), None))
    sizes = tuple(mesh.shape[a] for a in ("gx", "gy", "gz"))
    return jax.shard_map(
        functools.partial(per_device, sizes),
        mesh=mesh,
        in_specs=in_specs,
        out_specs=out_specs,
        check_vma=False,
    )
```

```python
import functools

import jax
import jax.numpy as jnp
from jax import lax
from jax.experimental import pallas as pl
from jax.experimental.pallas import tpu as pltpu
from jax.sharding import PartitionSpec as P

MESH = pl.DeviceIdType.MESH
SUBS = 24
EPS4 = 4e-6
F32 = jnp.float32
BF16 = jnp.bfloat16

OWN = 3 * 32
TOP = 19 * 32
FIELD = 21 * 32
COLUMN = 40 * 8


def weno_line(count, value, speed, emit):
    f_a, f_b, f_c, f_d = value(-3), value(-2), value(-1), value(0)
    d_prev, d_here, d_next = f_b - f_a, f_c - f_b, f_d - f_c
    half_here, half_next = 0.5 * f_c, 0.5 * f_d

    def smooth(e):
        return (13.0 / 3.0) * (e * e) + EPS4

    e_low, e_mid = d_here - d_prev, d_next - d_here
    q_low, q_mid = smooth(e_low), smooth(e_mid)
    t_low = e_mid - e_low
    f_last = f_d
    flux_prev = None
    for face in range(count + 1):
        f_new = value(face + 1)
        d_new = f_new - f_last
        e_high = d_new - d_next
        q_high = smooth(e_high)
        t_high = e_high - e_mid
        g_low = e_low + 2.0 * d_here
        g_mid = d_here + d_next
        g_high = e_high - 2.0 * d_next
        b_low = q_low + g_low * g_low
        b_mid = q_mid + g_mid * g_mid
        b_high = q_high + g_high * g_high
        w_low = b_mid * b_high
        w_mid = b_low * b_high
        w_high = b_low * b_mid
        w_low = w_low * w_low
        w_mid = w_mid * w_mid
        w_high = 0.5 * (w_high * w_high)
        num = w_low * ((1.0 / 3.0) * t_low) + w_high * t_high
        den = w_low + 6.0 * (w_mid + w_high)
        central = (half_here + half_next) - (1.0 / 6.0) * e_mid
        flux = speed(face) * (central - num * pl.reciprocal(den, approx=True))
        if face:
            emit(face - 1, flux - flux_prev)
        flux_prev = flux
        f_last = f_new
        half_here, half_next = half_next, 0.5 * f_new
        d_here, d_next = d_next, d_new
        e_low, e_mid = e_mid, e_high
        q_low, q_mid = q_mid, q_high
        t_low = t_high


def kernel(
    nx, ny, nz,
    mass_hbm, courant_hbm, rate_hbm, steps_hbm, gain_hbm, collide_hbm,
    out_ref, rain_ref,
    raw, courant_ref, rate_ref, steps_ref, gains, collide_ref, field, tend, x_low, x_high, x_out, y_low, y_high, y_out, y_in, winds,
    speed_x, speed_y, speed_z, taps, rain_taps, levels, stage, cells, rounded, rain, done, rain_done,
    load_sem, halo_send, halo_recv, wind_send, wind_recv, sed_send, sed_recv, rain_send, rain_recv,
    store_sem,
):
    gx, gy, gz = lax.axis_index("gx"), lax.axis_index("gy"), lax.axis_index("gz")
    parity = lax.rem(gz, 2)
    odd = parity == 1
    even = parity == 0
    near_half, far_half = 1 - parity, parity

    def when(cond, fn):
        pl.when(cond)(fn)

    sides = [
        (gx > 0, {"gx": lax.rem(gx + nx - 1, nx)}),
        (gx < nx - 1, {"gx": lax.rem(gx + 1, nx)}),
        (gy > 0, {"gy": lax.rem(gy + ny - 1, ny)}),
        (gy < ny - 1, {"gy": lax.rem(gy + 1, ny)}),
        (gz > 0, {"gz": lax.rem(gz + nz - 1, nz)}),
        (gz < nz - 1, {"gz": lax.rem(gz + 1, nz)}),
    ]

    barrier = pltpu.get_barrier_semaphore()
    for there, where in sides:
        when(
            there,
            lambda where=where: pl.semaphore_signal(
                barrier, inc=1, device_id=where, device_id_type=MESH
            ),
        )
    loads = [
        pltpu.make_async_copy(source, target, load_sem.at[k])
        for k, (source, target) in enumerate(
            (
                (mass_hbm, raw),
                (courant_hbm, courant_ref),
                (rate_hbm, rate_ref),
                (steps_hbm, steps_ref),
                (gain_hbm, gains),
                (collide_hbm, collide_ref),
            )
        )
    ]
    for load in loads:
        load.start()

    lane = lax.broadcasted_iota(jnp.int32, (8, 128), 1)
    low = lane < 64

    def turn(v):
        return pltpu.roll(v, 64, 1)

    def fill(ref, start, rows):
        ref[pl.ds(start, rows), :] = jnp.zeros((rows, 128), F32)

    def no_x_low():
        fill(x_low, 0, 384)
        fill(winds, 0, 8)

    def no_x_high():
        fill(x_high, 0, 256)
        fill(winds, 16, 8)

    def no_y_low():
        fill(y_in, 0, 384)
        fill(winds, 24, 8)

    def no_y_high():
        fill(y_in, 384, 256)
        fill(winds, 40, 8)

    def no_z_low():
        fill(field, 0, OWN)
        fill(field, FIELD, OWN)
        fill(winds, 48, 8)

    def no_z_high():
        fill(field, TOP, 64)
        fill(field, FIELD + TOP, 64)
        fill(winds, 64, 8)
        for yi in range(4):
            fill(levels, yi * COLUMN + 128, 128)

    for (there, _), fn in zip(
        sides, (no_x_low, no_x_high, no_y_low, no_y_high, no_z_low, no_z_high)
    ):
        when(jnp.logical_not(there), fn)
    def none_above():
        for yi in range(4):
            fill(levels, yi * COLUMN + 256, 64)

    when(gz >= nz - 2, none_above)

    loads[0].wait()

    def pack(z, carry):
        for yi in range(4):
            lo = raw[pl.ds(16 * yi + z, 8, stride=128), :]
            hi = raw[pl.ds(16 * (yi + 4) + z, 8, stride=128), :]
            field[pl.ds(pl.multiple_of(OWN + z * 32 + yi * 8, 8), 8), :] = jnp.concatenate(
                [lo, hi], axis=1
            )
        return carry

    lax.fori_loop(0, 16, pack, 0, unroll=8)

    loads[1].wait()
    for d in range(3):
        for y in range(8):
            winds[pl.ds(d * 24 + 8, 8), pl.ds(16 * y, 16)] = courant_ref[d, :, y, :]

    waits = jnp.int32(0)
    for there, _ in sides:
        waits = waits + there.astype(jnp.int32)
    pl.semaphore_wait(barrier, waits)

    def copy_of(src, dst, send, recv, where):
        return pltpu.make_async_remote_copy(
            src_ref=src, dst_ref=dst, send_sem=send, recv_sem=recv,
            device_id=where, device_id_type=MESH,
        )

    def halo(s, slot, to, src, dst):
        return (
            to,
            to ^ 1,
            copy_of(src, dst, halo_send.at[slot, to], halo_recv.at[slot, to], sides[to][1]),
        )

    def halos_xy(s, slot, half, halves):
        def at(start, rows):
            return pl.ds(pl.multiple_of(start + half * rows, 8), rows * halves)

        return [
            halo(s, slot, 0, x_out.at[at(s * 320 + 192, 64)], x_high.at[at(s * 128, 64)]),
            halo(s, slot, 1, x_out.at[at(s * 320, 96)], x_low.at[at(s * 192, 96)]),
            halo(s, slot, 2, y_out.at[at(s * 320 + 192, 64)], y_in.at[at(384 + s * 128, 64)]),
            halo(s, slot, 3, y_out.at[at(s * 320, 96)], y_in.at[at(s * 192, 96)]),
        ]

    def halos_z(s):
        base = s * FIELD
        return [
            halo(s, s, 4, field.at[pl.ds(base + OWN, 64)], field.at[pl.ds(base + TOP, 64)]),
            halo(s, s, 5, field.at[pl.ds(base + TOP - 96, 96)], field.at[pl.ds(base, 96)]),
        ]

    wind_copies = []
    for d in range(3):
        own = winds.at[pl.ds(d * 24 + 8, 8)]
        for to in (2 * d, 2 * d + 1):
            dst = winds.at[pl.ds(d * 24 + (16 if to == 2 * d else 0), 8)]
            wind_copies.append(
                (to, to ^ 1, copy_of(own, dst, wind_send.at[to], wind_recv.at[to], sides[to][1]))
            )

    def start(copies, only):
        for to, _, copy in copies:
            if to in only:
                when(sides[to][0], copy.start)

    def finish_recv(copies, only):
        for to, source, copy in copies:
            if source in only:
                when(sides[source][0], copy.wait_recv)

    def finish_send(copies):
        for to, _, copy in copies:
            when(sides[to][0], copy.wait_send)

    def by_parity(even_side, fn):
        when(even, lambda: fn((even_side,)))
        when(odd, lambda: fn((9 - even_side,)))

    def start_near(copies):
        by_parity(5, lambda only: start(copies, only))

    def start_far(copies):
        by_parity(4, lambda only: start(copies, only))

    def recv_near(copies):
        by_parity(5, lambda only: finish_recv(copies, only))

    def recv_far(copies):
        by_parity(4, lambda only: finish_recv(copies, only))

    def pack_x(s, half):
        base = s * FIELD + OWN + half * 256
        for k in range(3):
            x_out[pl.ds(pl.multiple_of(s * 320 + half * 96 + k * 32, 8), 32), :] = field[
                pl.ds(base + 5 + k, 32, stride=8), :
            ]
        for k in range(2):
            x_out[pl.ds(pl.multiple_of(s * 320 + 192 + half * 64 + k * 32, 8), 32), :] = field[
                pl.ds(base + k, 32, stride=8), :
            ]

    def pack_y(s, half):
        base = s * FIELD + OWN + half * 256
        for zi in range(4):
            here = base + zi * 32
            for k in range(3):
                lo = field[pl.ds(pl.multiple_of(here + (k + 1) * 8, 8), 8), :]
                hi = field[pl.ds(pl.multiple_of(here + 128 + (k + 1) * 8, 8), 8), :]
                at = s * 320 + half * 96 + (zi * 3 + k) * 8
                y_out[pl.ds(pl.multiple_of(at, 8), 8), :] = jnp.where(low, turn(lo), hi)
            for k in range(2):
                lo = field[pl.ds(pl.multiple_of(here + k * 8, 8), 8), :]
                hi = field[pl.ds(pl.multiple_of(here + 128 + k * 8, 8), 8), :]
                at = s * 320 + 192 + half * 64 + (zi * 2 + k) * 8
                y_out[pl.ds(pl.multiple_of(at, 8), 8), :] = jnp.where(low, lo, turn(hi))

    def unpack_y(s, half):
        base = s * FIELD + OWN + half * 256
        for zi in range(4):
            here = base + zi * 32
            for k in range(3):
                at = half * 96 + (zi * 3 + k) * 8
                got = y_in[pl.ds(pl.multiple_of(s * 192 + at, 8), 8), :]
                own_a = turn(field[pl.ds(pl.multiple_of(here + (k + 1) * 8, 8), 8), :])
                own_b = turn(field[pl.ds(pl.multiple_of(here + 128 + (k + 1) * 8, 8), 8), :])
                at = half * 192 + (zi * 3 + k) * 8
                y_low[pl.ds(pl.multiple_of(at, 8), 8), :] = jnp.where(low, got, own_a)
                y_low[pl.ds(pl.multiple_of(at + 96, 8), 8), :] = jnp.where(low, turn(got), own_b)
            for k in range(2):
                at = 384 + s * 128 + half * 64 + (zi * 2 + k) * 8
                got = y_in[pl.ds(pl.multiple_of(at, 8), 8), :]
                own_a = turn(field[pl.ds(pl.multiple_of(here + k * 8, 8), 8), :])
                own_b = turn(field[pl.ds(pl.multiple_of(here + 128 + k * 8, 8), 8), :])
                at = half * 128 + (zi * 2 + k) * 8
                y_high[pl.ds(pl.multiple_of(at, 8), 8), :] = jnp.where(low, own_a, turn(got))
                y_high[pl.ds(pl.multiple_of(at + 64, 8), 8), :] = jnp.where(low, own_b, got)

    def pass_x(s, half, fresh):
        base = s * FIELD + OWN

        def body(q, carry):
            at = half * 32 + q * 16

            def value(i):
                if i < 0:
                    row = s * 192 + half * 96 + (i + 3) * 32 + q * 16
                    return x_low[pl.ds(pl.multiple_of(row, 8), 16), :]
                if i > 7:
                    row = s * 128 + half * 64 + (i - 8) * 32 + q * 16
                    return x_high[pl.ds(pl.multiple_of(row, 8), 16), :]
                return field[pl.ds(base + at * 8 + i, 16, stride=8), :]

            def speed(k):
                return speed_x[pl.ds(pl.multiple_of(k * 64 + at, 8), 16), :]

            def emit(i, change):
                to = pl.ds(at * 8 + i, 16, stride=8)
                tend[to, :] = -change if fresh else tend[to, :] - change

            weno_line(8, value, speed, emit)
            return carry

        lax.fori_loop(0, 2, body, 0, unroll=2)

    def pass_y(s, first_level, count, last):
        base = s * FIELD + OWN

        def body(k, carry):
            z = first_level + k

            def value(i):
                if i < 0:
                    return y_low[pl.ds(pl.multiple_of((z * 3 + i + 3) * 8, 8), 8), :]
                if i > 3:
                    return y_high[pl.ds(pl.multiple_of((z * 2 + i - 4) * 8, 8), 8), :]
                return field[pl.ds(pl.multiple_of(base + z * 32 + i * 8, 8), 8), :]

            def speed(k):
                return speed_y[pl.ds(pl.multiple_of((z * 5 + k) * 8, 8), 8), :]

            def emit(i, change):
                row = z * 32 + i * 8
                at = pl.ds(pl.multiple_of(row, 8), 8)
                total = tend[at, :] - change
                if not last:
                    tend[at, :] = total
                    return
                stepped = value(i) + total
                if s == 0:
                    field[pl.ds(pl.multiple_of(FIELD + OWN + row, 8), 8), :] = stepped
                else:
                    before = field[pl.ds(pl.multiple_of(OWN + row, 8), 8), :]
                    to = pl.ds(pl.multiple_of(i * COLUMN + z * 8, 8), 8)
                    levels[to, :] = 0.5 * before + 0.5 * stepped

            weno_line(4, value, speed, emit)
            return carry

        unroll = 2 if count % 2 == 0 else 1
        lax.fori_loop(0, count, body, 0, unroll=unroll)

    def pass_z(s, first_level, count, last):
        for p in range(2):
            at = first_level * 32 + p * 16

            def value(i):
                return field[pl.ds(pl.multiple_of(s * FIELD + (i + 3) * 32 + at, 8), 16), :]

            def speed(k):
                return speed_z[pl.ds(pl.multiple_of(k * 32 + at, 8), 16), :]

            def emit(i, change):
                row = i * 32 + at
                if not last:
                    tend[pl.ds(pl.multiple_of(row, 8), 16), :] = -change
                    return
                stepped = value(i) + (tend[pl.ds(pl.multiple_of(row, 8), 16), :] - change)
                if s == 0:
                    field[pl.ds(pl.multiple_of(FIELD + OWN + row, 8), 16), :] = stepped
                else:
                    before = field[pl.ds(pl.multiple_of(OWN + row, 8), 16), :]
                    settled = 0.5 * before + 0.5 * stepped
                    for k in range(2):
                        to = (2 * p + k) * COLUMN + (first_level + i) * 8
                        levels[pl.ds(pl.multiple_of(to, 8), 8), :] = settled[8 * k : 8 * k + 8]

            weno_line(count, value, speed, emit)

    first_z, first_xy = halos_z(0), halos_xy(0, 0, 0, 2)
    start_far(first_z)
    start_far(wind_copies)
    start_near(first_z)
    start_near(wind_copies)
    start(wind_copies, (0, 1, 2, 3))
    for half in range(2):
        pack_y(0, half)
    start(first_xy, (2, 3))
    for half in range(2):
        pack_x(0, half)
    start(first_xy, (0, 1))

    column = jnp.where(low, 0, 64)

    def spread(v, index):
        return jnp.take_along_axis(v, index, axis=1)

    def speeds_x():
        right = 0.5 * (winds[pl.ds(8, 8), :] + winds[pl.ds(9, 8), :])
        left = jnp.broadcast_to(0.5 * (winds[pl.ds(7, 1), :] + winds[pl.ds(8, 1), :]), (8, 128))

        def body(z, carry):
            for yi in range(4):
                index = column + (16 * yi + z)
                row = z * 4 + yi
                speed_x[pl.ds(64 + row, 8, stride=64), :] = spread(right, index)
                speed_x[pl.ds(row, 1), :] = spread(left, index)[0:1, :]
            return carry

        lax.fori_loop(0, 16, body, 0, unroll=8)

    def speeds_y():
        own, before, after = (winds[pl.ds(24 + k, 8), :] for k in (8, 0, 16))
        following = jnp.where(lane < 112, pltpu.roll(own, 112, 1), pltpu.roll(after, 112, 1))
        right = 0.5 * (own + following)
        left = 0.5 * (own + pltpu.roll(before, 16, 1))

        def body(z, carry):
            first_face = jnp.where(
                low,
                spread(left, jnp.zeros_like(lane) + z),
                spread(right, jnp.zeros_like(lane) + (48 + z)),
            )
            speed_y[pl.ds(pl.multiple_of(z * 40, 8), 8), :] = first_face
            for k in range(1, 5):
                speed_y[pl.ds(pl.multiple_of(z * 40 + k * 8, 8), 8), :] = spread(
                    right, column + (16 * (k - 1) + z)
                )
            return carry

        lax.fori_loop(0, 16, body, 0, unroll=8)

    def speeds_z():
        own = winds[pl.ds(56, 8), :]
        right = 0.5 * (own + pltpu.roll(own, 127, 1))

        def body(z, carry):
            for yi in range(4):
                speed_z[pl.ds(pl.multiple_of(32 + z * 32 + yi * 8, 8), 8), :] = spread(
                    right, column + (16 * yi + z)
                )
            return carry

        lax.fori_loop(0, 15, body, 0, unroll=5)

    def speeds_bottom():
        left = 0.5 * (winds[pl.ds(56, 8), :] + pltpu.roll(winds[pl.ds(48, 8), :], 113, 1))
        for yi in range(4):
            speed_z[pl.ds(yi * 8, 8), :] = spread(left, column + 16 * yi)

    def speeds_top():
        right = 0.5 * (winds[pl.ds(56, 8), :] + pltpu.roll(winds[pl.ds(64, 8), :], 15, 1))
        for yi in range(4):
            speed_z[pl.ds(512 + yi * 8, 8), :] = spread(right, column + (16 * yi + 15))

    speeds_z()
    finish_recv(wind_copies, (0, 1))
    speeds_x()
    finish_recv(wind_copies, (2, 3))
    speeds_y()
    recv_near(wind_copies)
    when(even, speeds_top)
    when(odd, speeds_bottom)
    finish_recv(first_xy, (0, 1))
    for half in range(2):
        pass_x(0, half, True)
    finish_recv(first_xy, (2, 3))
    for half in range(2):
        unpack_y(0, half)
    pass_y(0, 0, 16, False)
    recv_near(first_z)
    pass_z(0, 3 * near_half, 13, True)

    second_z = halos_z(1)
    second_near = halos_xy(1, 1, near_half, 1)
    second_far = halos_xy(1, 2, far_half, 1)
    start_near(second_z)
    pack_y(1, near_half)
    start(second_near, (2, 3))
    pack_x(1, near_half)
    start(second_near, (0, 1))

    recv_far(wind_copies)
    when(even, speeds_bottom)
    when(odd, speeds_top)
    recv_far(first_z)
    pass_z(0, 13 * far_half, 3, True)
    start_far(second_z)
    pack_y(1, far_half)
    start(second_far, (2, 3))
    pack_x(1, far_half)
    start(second_far, (0, 1))

    def sed_copy(kind, yi):
        source, target = ((0, 16), (8, 24), (16, 32))[kind]
        return copy_of(
            levels.at[pl.ds(pl.multiple_of(yi * COLUMN + source * 8, 64), 64)],
            levels.at[pl.ds(pl.multiple_of(yi * COLUMN + target * 8, 64), 64)],
            sed_send.at[yi, kind], sed_recv.at[yi, kind], sides[4][1],
        )

    above = gz < nz - 1
    above_two = gz < nz - 2
    below = gz > 0
    hands_on = jnp.logical_and(below, above)

    def sed_start(kind):
        for yi in range(4):
            when(below, sed_copy(kind, yi).start)

    loads[2].wait()
    loads[3].wait()
    rates = jnp.concatenate([rate_ref[...], rate_ref[...]], axis=1)
    counts = jnp.concatenate([steps_ref[...], steps_ref[...]], axis=1)
    tap = (lax.broadcasted_iota(jnp.int32, (32, 128), 0) == 0).astype(F32)
    fallen = jnp.zeros((32, 128), F32)
    for s in range(SUBS):
        rate = jnp.where(s < counts, rates, 0.0)
        fallen = fallen + rate * tap
        tap = tap + rate * (pltpu.roll(tap, 1, 0) - tap)
    taps[...] = tap
    rain_taps[...] = fallen

    finish_recv(second_near, (0, 1))
    pass_x(1, near_half, True)
    finish_recv(second_near, (2, 3))
    unpack_y(1, near_half)
    pass_y(1, 8 * near_half, 8, False)
    recv_near(second_z)
    pass_z(1, 8 * near_half, 8, True)
    when(even, lambda: sed_start(1))
    when(odd, lambda: sed_start(0))

    finish_recv(second_far, (0, 1))
    pass_x(1, far_half, True)
    finish_recv(second_far, (2, 3))
    unpack_y(1, far_half)
    pass_y(1, 8 * far_half, 8, False)
    recv_far(second_z)
    pass_z(1, 8 * far_half, 8, True)

    def hand_on(u):
        for k in range(2):
            when(above, sed_copy(0, 2 * u + k).wait_recv)
            when(hands_on, sed_copy(2, 2 * u + k).start)

    def far_even():
        for yi in range(4):
            when(below, sed_copy(0, yi).start)
        for u in range(2):
            hand_on(u)

    when(even, far_even)
    when(odd, lambda: sed_start(1))

    def rain_copy(step):
        return copy_of(
            rain, rain, rain_send.at[step - 1], rain_recv.at[step - 1],
            {"gz": lax.rem(gz + step, nz)},
        )

    lowest = gz == 0
    sends_far = jnp.logical_and(even, above_two)
    follows = jnp.logical_and(even, gz > 0)

    def rain_make():
        def body(yi, carry):
            total = jnp.zeros((8, 128), F32)
            for m in range(SUBS):
                at = pl.ds(pl.multiple_of(yi * COLUMN + m * 8, 8), 8)
                total = total + rain_taps[pl.ds(m, 1), :] * levels[at, :]
            rain[pl.ds(pl.multiple_of(yi * 8, 8), 8), :] = total
            return carry

        lax.fori_loop(0, 4, body, 0)

    def rain_pass():
        rain_copy(1).start()
        when(sends_far, rain_copy(2).start)

    def rain_first():
        rain_make()
        rain_pass()

    def rain_forward():
        rain_copy(2).wait_recv()
        rain_pass()

    when(lowest, rain_first)

    loads[4].wait()
    loads[5].wait()

    def settle(u, group):
        def body(k2, carry):
            base = pl.multiple_of((2 * u + k2) * COLUMN + group * 64, 64)
            sums = [None] * 8
            for j in range(8 + SUBS):
                v = levels[pl.ds(base + j * 8, 8), :]
                for k in range(8):
                    if 0 <= j - k <= SUBS:
                        term = taps[pl.ds(j - k, 1), :] * v
                        sums[k] = term if sums[k] is None else sums[k] + term
            for k in range(8):
                stage[pl.ds(pl.multiple_of(k2 * 64 + k * 8, 8), 8), :] = sums[k]
            return carry

        lax.fori_loop(0, 2, body, 0, unroll=2)

    def breakup(u, group):
        block = jnp.concatenate(
            [stage[pl.ds(k2 * 64 + x, 8, stride=8), :] for k2 in range(2) for x in range(8)], axis=0
        ).T
        for h in range(2):
            cells[:, 128 * h : 128 * h + 128] = block[64 * h : 64 * h + 64]
        small = cells[...].astype(BF16)
        rounded[...] = small.astype(F32)

        def body(i, total):
            wide = rounded[...]
            terms = [rounded[pl.ds(i * 4 + k, 1), :] * wide for k in range(4)]
            block = jnp.concatenate(terms, axis=0).astype(BF16)
            part = gains[:, pl.ds(pl.multiple_of(i * 256, 256), 256)]
            return total + jnp.dot(part, block, preferred_element_type=F32)

        loss = lax.dot_general(
            collide_ref[...], small, (((0,), (0,)), ((), ())), preferred_element_type=F32
        )
        gained = lax.fori_loop(0, 16, body, jnp.zeros((64, 256), F32), unroll=16)
        settled = cells[...]
        result = settled + gained - settled * loss
        for h in range(2):
            back = result[:, 128 * h : 128 * h + 128].T
            for k2 in range(2):
                done[
                    :, pl.ds(4 * h + 2 * u + k2, 1), pl.ds(pl.multiple_of(8 * group, 8), 8), :
                ] = back[64 * k2 : 64 * k2 + 64].reshape(8, 1, 8, 64)

    def unit_of(t):
        outer, inner = t // 2, t % 2
        return parity * outer + (1 - parity) * inner, parity * inner + (1 - parity) * outer

    def store(t, h):
        u, group = unit_of(t)
        where = (
            slice(None),
            pl.ds(4 * h + 2 * u, 2),
            pl.ds(pl.multiple_of(8 * group, 8), 8),
            slice(None),
        )
        return pltpu.make_async_copy(done.at[where], out_ref.at[where], store_sem.at[t, h])

    def both(a, b):
        return jnp.logical_and(a, b)

    for t in range(4):
        u, group = unit_of(t)
        if t % 2 == 0:
            when(odd, lambda u=u: hand_on(u))
        for k in range(2):
            when(both(group == 0, above), sed_copy(1, 2 * u + k).wait_recv)
        if t == 2:
            when(follows, rain_forward)
        for k in range(2):
            when(both(group == 1, above_two), sed_copy(2, 2 * u + k).wait_recv)
        settle(u, group)
        breakup(u, group)
        for h in range(2):
            store(t, h).start()

    when(odd, rain_copy(1).wait_recv)
    mine = rain[pl.ds(pl.multiple_of(lax.rem(gz, 4) * 8, 8), 8), :]
    upper = (jnp.zeros((8, 128), jnp.int32) + gz) >= 4
    rain_done[:, 0, :] = jnp.where(upper, turn(mine), mine)[:, :64]
    rain_store = pltpu.make_async_copy(rain_done, rain_ref, load_sem.at[0])
    rain_store.start()

    when(even, rain_copy(1).wait_send)
    when(sends_far, rain_copy(2).wait_send)
    for yi in range(4):
        when(below, sed_copy(0, yi).wait_send)
        when(below, sed_copy(1, yi).wait_send)
        when(hands_on, sed_copy(2, yi).wait_send)
    finish_send(wind_copies)
    for t in range(4):
        for h in range(2):
            store(t, h).wait()
    rain_store.wait()
    for copies in (first_z, first_xy, second_z, second_near, second_far):
        finish_send(copies)


def hand_over(mass_ref, fall_ref, out_ref, rain_ref, mass, fall, sem):
    reads = [pltpu.make_async_copy(fall_ref, fall, sem.at[0, 8])]
    writes = [pltpu.make_async_copy(fall, rain_ref, sem.at[1, 8])]
    for k in range(8):
        reads.append(pltpu.make_async_copy(mass_ref.at[k], mass.at[k], sem.at[0, k]))
        writes.append(pltpu.make_async_copy(mass.at[k], out_ref.at[k], sem.at[1, k]))
    for copy in reads:
        copy.start()
    for read, write in zip(reads, writes):
        read.wait()
        write.start()
    for copy in writes:
        copy.wait()


def per_device(sizes, bin_mass, courant, sub_courant, fall_steps, frag_gain, collide):
    vmem, dma = pltpu.VMEM, pltpu.SemaphoreType.DMA
    out, rain = pl.pallas_call(
        functools.partial(kernel, *sizes),
        out_shape=(
            jax.ShapeDtypeStruct((8, 8, 16, 64), F32),
            jax.ShapeDtypeStruct((8, 1, 64), F32),
        ),
        in_specs=[pl.BlockSpec(memory_space=pl.ANY)] * 6,
        out_specs=(pl.BlockSpec(memory_space=pl.ANY), pl.BlockSpec(memory_space=pl.ANY)),
        scratch_shapes=[
            vmem((1024, 64), F32),
            vmem((3, 8, 8, 16), F32),
            vmem((1, 64), F32),
            vmem((1, 64), jnp.int32),
            vmem((64, 4096), BF16),
            vmem((64, 64), BF16),
            vmem((2 * FIELD, 128), F32),
            vmem((512, 128), F32),
            vmem((384, 128), F32),
            vmem((256, 128), F32),
            vmem((640, 128), F32),
            vmem((384, 128), F32),
            vmem((256, 128), F32),
            vmem((640, 128), F32),
            vmem((640, 128), F32),
            vmem((72, 128), F32),
            vmem((9 * 64, 128), F32),
            vmem((16 * 40, 128), F32),
            vmem((17 * 32, 128), F32),
            vmem((32, 128), F32),
            vmem((32, 128), F32),
            vmem((4 * COLUMN, 128), F32),
            vmem((128, 128), F32),
            vmem((64, 256), F32),
            vmem((64, 256), F32),
            vmem((32, 128), F32),
            vmem((8, 8, 16, 64), F32),
            vmem((8, 1, 64), F32),
            dma((6,)),
            dma((3, 6)),
            dma((3, 6)),
            dma((6,)),
            dma((6,)),
            dma((4, 3)),
            dma((4, 3)),
            dma((2,)),
            dma((2,)),
            dma((4, 2)),
        ],
        compiler_params=pltpu.CompilerParams(
            collective_id=0, has_side_effects=True, vmem_limit_bytes=60 << 20
        ),
    )(
        bin_mass.reshape(1024, 64),
        courant,
        sub_courant.reshape(1, 64),
        fall_steps.reshape(1, 64),
        frag_gain.T,
        collide,
    )
    return pl.pallas_call(
        hand_over,
        out_shape=(
            jax.ShapeDtypeStruct((8, 8, 16, 64), F32),
            jax.ShapeDtypeStruct((8, 1, 64), F32),
        ),
        in_specs=[pl.BlockSpec(memory_space=pl.ANY)] * 2,
        out_specs=(pl.BlockSpec(memory_space=pl.ANY), pl.BlockSpec(memory_space=pl.ANY)),
        scratch_shapes=[vmem((8, 8, 16, 64), F32), vmem((8, 1, 64), F32), dma((2, 9))],
        compiler_params=pltpu.CompilerParams(vmem_limit_bytes=60 << 20),
    )(out, rain)


def solution(mesh):
    in_specs = (P("gx", "gy", "gz", None), P(None, "gx", "gy", "gz"), P(), P(), P(), P())
    out_specs = (P("gx", "gy", "gz", None), P("gx", ("gy", "gz"), None))
    sizes = tuple(mesh.shape[a] for a in ("gx", "gy", "gz"))
    return jax.shard_map(
        functools.partial(per_device, sizes),
        mesh=mesh,
        in_specs=in_specs,
        out_specs=out_specs,
        check_vma=False,
    )
```
